512 devices in a mesh: inst: 8 (over y), tm: 16 (over z, core), filt: 4 (over x).
Axes of the slice: x: 4, y: 8, z: 8, core: 2. Of those that a mesh axis runs over, the one named last changes fastest.
Arguments:
- activations: bfloat16 [32, 7680, 256], P('inst', 'tm'), may hold values from -6 to 6
- conv_weight: bfloat16 [2304, 512], P(None, 'filt'), may hold values from -0.125 to 0.125
- class_weight: float32 [512, 5], P('filt'), may hold values from -1.2 to 1.2
- class_bias: float32 [5], replicated, may hold values from -4 to 4
- teacher_logits: float32 [32, 64, 5], P('inst', 'tm'), may hold values from -15 to 300
- night_of: int32 [32], P('inst'), may hold values from 0 to 7, never falling along the last dimension, each value on 1 to 8 neighbouring positions
- section_labels: int32 [8, 64], P(None, 'tm'), may hold values from 0 to 4
Outputs:
- student_logits: float32 [32, 64, 5], P('inst', 'tm')
- grad_weight: float32 [2304, 512], P(('inst', 'tm'), 'filt')
The draws below stay inside these ranges and needn't reach their ends.
Inputs may be any that keep to these rules, and one draw needn't show every extreme that they name: `night_of`: instances of one night stand in a row, each night has 1 to 8 of them and some night has 8.
All inputs are finite; a program needn't handle non-finite values.
Results may differ from the reference program's by a relative error of at most 0.0011.
Values may be sent and summed in bfloat16 or wider, within the bound.
A program may use at most 64 MiB of HBM per device.

```python
import math
import jax
import jax.numpy as jnp
import numpy as np
from jax import lax

C = 256
F = 512
TAPS = 9
EPOCH = 120
S = 5
INSTANCES = 32
NIGHTS = 8
MOST = 8
TL = 7680
EPOCHS = 64


def draw_teacher_logits(key, part):
    key = jax.random.fold_in(key, 11)
    keys = jax.random.split(key, 7)
    shape = (INSTANCES, EPOCHS, S)
    values = jnp.clip(3.0 * jax.random.normal(keys[6], shape, jnp.float32), -15.0, 15.0)
    return values.astype(jnp.float32)


def place_ends(entries, stream_key, low, largest):
    shape = entries.shape
    spot = [jax.random.randint(jax.random.fold_in(stream_key, axis), (), 0, shape[axis]) for axis in range(len(shape))]
    entries = entries.at[tuple(spot)].set(low)
    longest = shape.index(max(shape))
    spot[longest] = (spot[longest] + 1) % shape[longest]
    return entries.at[tuple(spot)].set(largest)


def steps_of(key, dims, shards, smallest, top_value):
    def one(axis_at, blocks):
        steps = jax.random.uniform(jax.random.fold_in(jax.random.fold_in(key, 6), axis_at), (blocks,), jnp.float32, smallest / len(shards), top_value / len(shards))
        return jnp.repeat(jnp.exp(steps), dims[axis_at] // blocks).reshape((-1,) + (1,) * (len(dims) - axis_at - 1))

    level = one(*shards[0])
    for cut in shards[1:]:
        level = level * one(*cut)
    return level


def split_up(number_of, total, limit, lean):
    loads = [(1 << 20) // math.isqrt(grade ** lean) + 1 for grade in range(2, number_of + 1)]
    surplus, given = total - limit - (number_of - 1), [1] * (number_of - 1)
    while surplus > 0:
        free = [i for i in range(number_of - 1) if given[i] < limit]
        whole, budget = sum([loads[i] for i in free]), surplus
        for i in free:
            more = min(limit - given[i], max(1, budget * loads[i] // whole), surplus)
            given[i] = given[i] + more
            surplus = surplus - more
    return np.array([limit] + given)


def uneven(rng, number_of, total, limit, skew):
    if number_of == 2:
        one = jax.random.randint(rng, (), max(1, total - limit), min(limit, total - 1) + 1)
        return jnp.stack([one, total - one])
    sizes = jnp.asarray(split_up(number_of, total, limit, skew), jnp.int32)
    pairs = (number_of - 1) // 2
    giver, sink = sizes[1:1 + 2 * pairs:2], sizes[2:2 + 2 * pairs:2]
    slack = jnp.minimum(giver - 1, limit - sink)
    shifted = jax.random.randint(jax.random.fold_in(rng, 1), (pairs,), 0, 1 << 20) % (slack + 1)
    sizes = sizes.at[1:1 + 2 * pairs:2].set(giver - shifted).at[2:2 + 2 * pairs:2].set(sink + shifted)
    return sizes[jax.random.permutation(jax.random.fold_in(rng, 2), number_of)]


def gaussian(own_key, shape, deviation, reach, cuts=(), kind=jnp.bfloat16):
    entries = deviation * jax.random.normal(own_key, shape, jnp.float32)
    if cuts:
        entries = entries * steps_of(own_key, shape, cuts, -0.22, 0.18)
    return jnp.clip(entries, -reach, reach).astype(kind)


def setup_inputs(seed: int = 0) -> dict:
    key_of = jax.random.split(jax.random.key(seed), 8)
    activations = gaussian(key_of[0], (INSTANCES, TL, C), 1.0, 6.0, ((0, 8), (1, 16)))
    conv_weight = gaussian(key_of[1], (TAPS * C, F), (TAPS * C) ** -0.5, 0.125, ((1, 4),))
    class_weight = gaussian(key_of[2], (F, S), 0.2, 1.2, ((0, 4),), jnp.float32)
    class_bias = gaussian(key_of[3], (S,), 1.0, 4.0, (), jnp.float32)
    teacher_logits = draw_teacher_logits(jax.random.fold_in(key_of[7], 71), 0)
    night_of = jnp.searchsorted(jnp.cumsum(uneven(key_of[5], NIGHTS, INSTANCES, MOST, 2)), jnp.arange(INSTANCES), side="right").astype(jnp.int32)
    section_labels = place_ends(jax.random.randint(key_of[6], (NIGHTS, EPOCHS), 0, S), jax.random.fold_in(key_of[6], 1), 0, S - 1).astype(jnp.int32)
    return dict(activations=activations, conv_weight=conv_weight, class_weight=class_weight, class_bias=class_bias, teacher_logits=teacher_logits, night_of=night_of, section_labels=section_labels)


def reference(activations, conv_weight, class_weight, class_bias, teacher_logits, night_of, section_labels):
    inst_rows = activations.shape[0]
    time_rows = activations.shape[1]
    margin = TAPS // 2
    kernel = conv_weight.reshape(TAPS, C, F)
    padded = jnp.pad(activations, ((0, 0), (margin, margin), (0, 0)))
    flat_rows = inst_rows * time_rows
    summed = jnp.zeros((flat_rows, F), jnp.float32)
    for offset in range(TAPS):
        window = padded[:, offset:offset + time_rows, :].reshape(flat_rows, C)
        summed = summed + jnp.dot(window, kernel[offset], preferred_element_type=jnp.float32)
    pre = summed.reshape(inst_rows, time_rows, F)
    act = jnp.where(pre > 0, pre, jnp.expm1(pre))
    epoch_count = time_rows // EPOCH
    pooled = act.reshape(inst_rows, epoch_count, EPOCH, F).mean(axis=2)
    logits = jnp.einsum('ief,fs->ies', pooled, class_weight, precision=lax.Precision.HIGHEST) + class_bias
    teacher = jax.nn.softmax(teacher_logits, axis=-1)
    member = (night_of[:, None] == jnp.arange(NIGHTS, dtype=jnp.int32)[None, :]).astype(jnp.float32)
    totals = jnp.einsum('in,ies->nes', member, teacher, precision=lax.Precision.HIGHEST)
    counts = jnp.sum(member, axis=0)
    ensemble = totals / counts[:, None, None]
    soft_target = jnp.einsum('in,nes->ies', member, ensemble, precision=lax.Precision.HIGHEST)
    label_hot = (section_labels[:, :, None] == jnp.arange(S, dtype=jnp.int32)[None, None, :]).astype(jnp.float32)
    hard_target = jnp.einsum('in,nes->ies', member, label_hot, precision=lax.Precision.HIGHEST)
    target = 0.5 * soft_target + 0.5 * hard_target
    expo = jnp.exp(logits)
    student = expo / jnp.sum(expo, axis=-1, keepdims=True)
    slope = jnp.einsum('ies,fs->ief', student - target, class_weight, precision=lax.Precision.HIGHEST)
    spread = jnp.broadcast_to(slope[:, :, None, :], (inst_rows, epoch_count, EPOCH, F)).reshape(inst_rows, time_rows, F)
    deriv = jnp.where(pre > 0, 1.0, jnp.exp(pre))
    upstream = (spread * deriv).astype(jnp.bfloat16).reshape(flat_rows, F)
    grads = []
    for offset in range(TAPS):
        window = padded[:, offset:offset + time_rows, :].reshape(flat_rows, C)
        grads.append(jnp.einsum('rc,rf->cf', window, upstream, preferred_element_type=jnp.float32))
    grad_weight = jnp.concatenate(grads, axis=0) / inst_rows
    return logits, grad_weight
```

```python
import functools

import jax
import jax.numpy as jnp
from jax import lax
from jax.experimental import pallas as pl
from jax.experimental.pallas import tpu as pltpu
from jax.sharding import PartitionSpec as P

f32, bf16, i32, i16 = jnp.float32, jnp.bfloat16, jnp.int32, jnp.int16
MESH = pl.DeviceIdType.MESH
EPOCH = 120
PAD = 16
UNIT = 36
WIDE = 2 * UNIT
WIDE_PAD = 80
SIXTEEN = False


def kernel(
    x, w, cw, tl, night, labels, bias,
    logits_out, grad_out,
    xp, wv, y_taps, deriv, pooled, up, xt, grad,
    teach, logit, half_tx, half_rx, total, tx, rx, piece, tx2, rx2,
    load_sem, halo_send, halo_recv, teach_send, teach_recv, logit_send, logit_recv,
    half_send, half_recv, send1, recv1, send2, recv2,
):
    yy, tm, xx = lax.axis_index("inst"), lax.axis_index("tm"), lax.axis_index("filt")
    zz, cc = tm // 2, tm % 2
    oc = 1 - cc
    ny, nz, nx = 8, 8, 4

    def remote(src, dst, ssem, rsem, dev):
        return pltpu.make_async_remote_copy(
            src_ref=src, dst_ref=dst, send_sem=ssem, recv_sem=rsem, device_id=dev, device_id_type=MESH
        )

    def arrived(dst, rsem):
        remote(dst, dst, rsem, rsem, (yy, tm, xx)).wait_recv()

    loads = [pltpu.make_async_copy(w, wv, load_sem.at[4])]
    loads += [
        pltpu.make_async_copy(x.at[i], xp.at[i, pl.ds(PAD, 480)], load_sem.at[i]) for i in range(4)
    ]
    for c in loads:
        c.start()

    barrier = pltpu.get_barrier_semaphore()

    def greet(dev):
        pl.semaphore_signal(barrier, inc=1, device_id=dev, device_id_type=MESH)

    greet((yy, zz * 2 + oc, xx))
    for d in range(1, 8):
        for c in range(2):
            greet((yy, lax.rem(zz + d, nz) * 2 + c, xx))
            greet((lax.rem(yy + d, ny), zz * 2 + c, xx))
    for d in range(1, 4):
        greet((yy, tm, lax.rem(xx + d, nx)))

    row = lax.broadcasted_iota(i32, (16, 128), 0)
    lane = lax.broadcasted_iota(i32, (16, 128), 1)
    t5 = jnp.concatenate([tl[i] for i in range(4)], axis=0)
    t5 = jnp.exp(t5 - jnp.max(t5, axis=1, keepdims=True))
    t5 = t5 / jnp.sum(t5, axis=1, keepdims=True)
    tile = jnp.zeros((16, 128), f32)
    for s in range(5):
        tile = jnp.where(lane == s, t5[:, s : s + 1], tile)
    for i in range(4):
        tile = jnp.where((lane == 8) & (row // 4 == i), night[i].astype(f32), tile)
    tile = jnp.where(lane == 9, 1.0, tile)
    teach[yy] = tile

    @pl.when(tm == 0)
    def _():
        for i in range(4):
            xp[i, 0:PAD, :] = jnp.zeros((PAD, 256), bf16)

    @pl.when(tm == 15)
    def _():
        for i in range(4):
            xp[i, PAD + 480 :, :] = jnp.zeros((PAD, 256), bf16)

    def weights(p):
        if p == 4:
            return wv[pl.ds(2048, 256), :]
        return jnp.concatenate([wv[pl.ds(512 * p, 256), :], wv[pl.ds(512 * p + 256, 256), :]], axis=1)

    def forward(i):
        for p in range(5):
            y = jnp.dot(xp[i, PAD : PAD + 480, :], weights(p), preferred_element_type=f32)
            y_taps[i, 2 * p, PAD : PAD + 480, :] = y[:, :128]
            if p < 4:
                y_taps[i, 2 * p + 1, PAD : PAD + 480, :] = y[:, 128:]

    loads[0].wait()
    loads[1].wait()
    forward(0)
    pl.semaphore_wait(barrier, 32)

    up_halo = remote(
        x.at[:, pl.ds(480 - PAD, PAD)], xp.at[:, pl.ds(0, PAD)], halo_send.at[0], halo_recv.at[0], (yy, tm + 1, xx)
    )
    down_halo = remote(
        x.at[:, pl.ds(0, PAD)], xp.at[:, pl.ds(PAD + 480, PAD)], halo_send.at[1], halo_recv.at[1], (yy, tm - 1, xx)
    )
    pl.when(tm < 15)(up_halo.start)
    pl.when(tm > 0)(down_halo.start)
    teach_copies = [
        remote(teach.at[yy], teach.at[yy], teach_send.at[d - 1], teach_recv.at[yy], (lax.rem(yy + d, ny), tm, xx))
        for d in range(1, 8)
    ]
    for c in teach_copies:
        c.start()

    for i in range(1, 4):
        loads[1 + i].wait()
        forward(i)

    pl.when(tm > 0)(up_halo.wait_recv)
    pl.when(tm < 15)(down_halo.wait_recv)
    xh = jnp.concatenate([xp[i, r : r + PAD, :] for i in range(4) for r in (0, PAD + 480)], axis=0)
    for p in range(5):
        y = jnp.dot(xh, weights(p), preferred_element_type=f32)
        for i in range(4):
            for h, r in enumerate((0, PAD + 480)):
                o = (2 * i + h) * PAD
                y_taps[i, 2 * p, r : r + PAD, :] = y[o : o + PAD, :128]
                if p < 4:
                    y_taps[i, 2 * p + 1, r : r + PAD, :] = y[o : o + PAD, 128:]

    for i in range(4):
        for e in range(4):
            o = PAD - 4 + EPOCH * e
            pre = y_taps[i, 0, pl.ds(o, EPOCH), :]
            for k in range(1, 9):
                pre = pre + y_taps[i, k, pl.ds(o + k, EPOCH), :]
            ex = jnp.exp(jnp.minimum(pre, 0.0))
            act = jnp.where(pre > 0, pre, ex - 1.0)
            deriv[i, pl.ds(EPOCH * e, EPOCH), :] = ex
            pooled[pl.ds(4 * i + e, 1), :] = jnp.sum(act, axis=0, keepdims=True) * (1.0 / EPOCH)

    cwt = cw[...]
    pool = pooled[...]
    part = jnp.zeros((16, 128), f32)
    for s in range(5):
        part = jnp.where(lane == s, jnp.sum(pool * cwt[s : s + 1, :], axis=1, keepdims=True), part)
    logit[xx] = part
    logit_copies = [
        remote(logit.at[xx], logit.at[xx], logit_send.at[d - 1], logit_recv.at[xx], (yy, tm, lax.rem(xx + d, nx)))
        for d in range(1, 4)
    ]
    for c in logit_copies:
        c.start()

    for i in range(4):
        xt[:, 512 * i : 512 * i + 512] = xp[i].T
    for d in range(1, 8):
        s = lax.rem(yy + d, ny)
        arrived(teach.at[s], teach_recv.at[s])
    nights = [night[i].astype(f32) for i in range(4)]
    sums = [jnp.zeros((16, 128), f32) for _ in range(4)]
    for j in range(8):
        t = teach[j]
        of = jnp.broadcast_to(t[:, 8:9], (16, 128))
        for i in range(4):
            sums[i] = sums[i] + jnp.where(of == nights[i], t, 0.0)
    soft = []
    for i in range(4):
        s = sums[i][0:4] + sums[i][4:8] + sums[i][8:12] + sums[i][12:16]
        soft.append(s / s[:, 9:10])
    soft = jnp.concatenate(soft, axis=0)
    label = jnp.zeros((16, 128), i32)
    for i in range(4):
        for e in range(4):
            label = jnp.where(row == 4 * i + e, labels[e, night[i]], label)
    target = 0.5 * soft + 0.5 * (lane == label).astype(f32)

    for d in range(1, 4):
        s = lax.rem(xx + d, nx)
        arrived(logit.at[s], logit_recv.at[s])
    logits = logit[0] + logit[1] + logit[2] + logit[3]
    for s in range(5):
        logits = logits + jnp.where(lane == s, bias[s], 0.0)
    for i in range(4):
        logits_out[i] = logits[4 * i : 4 * i + 4, :5]
    expo = jnp.where(lane < 5, jnp.exp(logits), 0.0)
    diff = expo / jnp.sum(expo, axis=1, keepdims=True) - target
    slope = jnp.zeros((16, 128), f32)
    for s in range(5):
        slope = slope + diff[:, s : s + 1] * cwt[s : s + 1, :]

    for i in range(4):
        up[i, 0:24, :] = jnp.zeros((24, 128), f32)
        up[i, 504:528, :] = jnp.zeros((24, 128), f32)
        for e in range(4):
            up[i, pl.ds(24 + EPOCH * e, EPOCH), :] = (
                deriv[i, pl.ds(EPOCH * e, EPOCH), :] * slope[4 * i + e : 4 * i + e + 1, :]
            )
    for p in range(5):
        acc = None
        for i in range(4):
            us = [up[i, pl.ds(12 - k, 512), :].astype(bf16) for k in range(2 * p, min(2 * p + 2, 9))]
            u = jnp.concatenate(us, axis=1) if p < 4 else us[0]
            g = jnp.dot(xt[:, 512 * i : 512 * i + 512], u, preferred_element_type=f32)
            acc = g if acc is None else acc + g
        grad[pl.ds(512 * p, 256), :] = acc[:, :128]
        if p < 4:
            grad[pl.ds(512 * p + 256, 256), :] = acc[:, 128:]

    def rows_of(j, h, core):
        if j < 8:
            return pl.ds(pl.multiple_of(core * 144, 8) + 288 * j + UNIT * (j % 2 + 2 * h), UNIT)
        z = j - 8
        return pl.ds(pl.multiple_of(core * 1152, 8) + 288 * (1 - z % 2 + 2 * h) + UNIT * z, UNIT)

    partner = (yy, zz * 2 + oc, xx)
    half_copies = []
    for part_at in range(2):
        for j in range(8 * part_at, 8 * part_at + 8):
            for h in range(2):
                half_tx[j, UNIT * h : UNIT * h + UNIT, :] = grad[rows_of(j, h, oc), :]
        sl = pl.ds(8 * part_at, 8)
        c = remote(half_tx.at[sl], half_rx.at[sl], half_send.at[part_at], half_recv.at[part_at], partner)
        c.start()
        half_copies.append(c)

    copies1 = []
    for part_at in range(2):
        half_copies[part_at].wait_recv()
        top = jnp.zeros((WIDE, 128), f32)
        for j in range(8 * part_at, 8 * part_at + 8):
            t = half_rx[j] + jnp.concatenate([grad[rows_of(j, h, cc), :] for h in range(2)], axis=0)
            total[j] = t
            top = jnp.maximum(top, jnp.abs(t))
        if SIXTEEN:
            top = jnp.max(top, axis=0, keepdims=True)
            power = jnp.ceil(jnp.log2(jnp.maximum(top, 1e-30)) + 0.01)
            factor = jnp.exp2(15.0 - power)
            power = jnp.broadcast_to(power, (WIDE_PAD - WIDE, 128))
            for j in range(8 * part_at, 8 * part_at + 8):
                q = jnp.concatenate([jnp.round(total[j] * factor), power], axis=0)
                tx[j] = q.astype(i32).astype(i16)
        else:
            for j in range(8 * part_at, 8 * part_at + 8):
                tx[j] = total[j]
        for d in range(1, 8):
            if part_at == 0:
                to, me = lax.rem(yy + d, ny), yy
                dev = (to, tm, xx)
            else:
                to, me = lax.rem(zz + d, nz), zz
                dev = (yy, to * 2 + cc, xx)
            base = 8 * part_at
            c = remote(
                tx.at[base + to], rx.at[base + me], send1.at[7 * part_at + d - 1], recv1.at[base + me], dev
            )
            c.start()
            copies1.append(c)

    copies2 = []
    for part_at in range(2):
        base = 8 * part_at
        me = yy if part_at == 0 else zz
        acc = total[base + me]
        for d in range(1, 8):
            s = base + lax.rem(me + d, 8)
            arrived(rx.at[s], recv1.at[s])
            t = rx[s].astype(f32)
            if SIXTEEN:
                t = t[:WIDE] * jnp.exp2(t[WIDE : WIDE + 1] - 15.0)
            acc = acc + t
        piece[part_at, 0:WIDE, :] = acc
        piece[part_at, WIDE:, :] = jnp.zeros((WIDE_PAD - WIDE, 128), f32)
        for m in range(4):
            tx2[4 * part_at + m] = piece[part_at, pl.ds(18 * m, 24), :]
        for m in range(4):
            h, c = m // 2, m % 2
            slot = 4 * part_at + m
            if part_at == 0:
                to, own = yy % 2 + 4 * cc + 2 * h, zz
                dev = (yy, to * 2 + c, xx)
                mine = (to == zz) & (cc == c)
            else:
                to, own = 4 * cc + 1 - zz % 2 + 2 * h, yy
                dev = (to, zz * 2 + c, xx)
                mine = (to == yy) & (cc == c)
            copy = remote(tx2.at[slot], rx2.at[own], send2.at[slot], recv2.at[own], dev)
            copies2.append((copy, mine))

            @pl.when(mine)
            def _():
                rx2[own] = tx2[slot]

            @pl.when(jnp.logical_not(mine))
            def _():
                copy.start()

    even = (yy + zz) % 2 == 0
    holder = jnp.where(even, zz // 4, yy // 4)
    place = jnp.where(even, zz, yy)
    for s in range(8):
        @pl.when(jnp.logical_not((place == s) & (holder == cc)))
        def _():
            arrived(rx2.at[s], recv2.at[s])
    out = rx2[0]
    for s in range(1, 8):
        out = out + rx2[s]
    grad_out[...] = out[:18] * (1.0 / 32)

    pl.when(tm < 15)(up_halo.wait_send)
    pl.when(tm > 0)(down_halo.wait_send)
    for c in teach_copies + logit_copies + half_copies + copies1:
        c.wait_send()
    for c, mine in copies2:
        pl.when(jnp.logical_not(mine))(c.wait_send)


def local(activations, conv_weight, class_weight, class_bias, teacher_logits, night_of, section_labels):
    vm = pl.BlockSpec(memory_space=pltpu.VMEM)
    sm = pl.BlockSpec(memory_space=pltpu.SMEM)
    hbm = pl.BlockSpec(memory_space=pltpu.HBM)
    wire, wire_rows = (i16, WIDE_PAD) if SIXTEEN else (f32, WIDE)
    dma = pltpu.SemaphoreType.DMA
    return pl.pallas_call(
        kernel,
        out_shape=(jax.ShapeDtypeStruct((4, 4, 5), f32), jax.ShapeDtypeStruct((18, 128), f32)),
        in_specs=[hbm, hbm, vm, vm, sm, sm, sm],
        out_specs=(vm, vm),
        scratch_shapes=[
            pltpu.VMEM((4, 512, 256), bf16),
            pltpu.VMEM((2304, 128), bf16),
            pltpu.VMEM((4, 9, 512, 128), f32),
            pltpu.VMEM((4, 480, 128), f32),
            pltpu.VMEM((16, 128), f32),
            pltpu.VMEM((4, 528, 128), f32),
            pltpu.VMEM((256, 2048), bf16),
            pltpu.VMEM((2304, 128), f32),
            pltpu.VMEM((8, 16, 128), f32),
            pltpu.VMEM((4, 16, 128), f32),
            pltpu.VMEM((16, WIDE, 128), f32),
            pltpu.VMEM((16, WIDE, 128), f32),
            pltpu.VMEM((16, WIDE, 128), f32),
            pltpu.VMEM((16, wire_rows, 128), wire),
            pltpu.VMEM((16, wire_rows, 128), wire),
            pltpu.VMEM((2, WIDE_PAD, 128), f32),
            pltpu.VMEM((8, 24, 128), f32),
            pltpu.VMEM((8, 24, 128), f32),
            dma((5,)),
            dma((2,)), dma((2,)),
            dma((7,)), dma((8,)),
            dma((3,)), dma((4,)),
            dma((2,)), dma((2,)),
            dma((14,)), dma((16,)),
            dma((8,)), dma((8,)),
        ],
        compiler_params=pltpu.CompilerParams(
            collective_id=0, has_side_effects=True, vmem_limit_bytes=48 << 20
        ),
    )(activations, conv_weight, class_weight.T, teacher_logits, night_of, section_labels.T, class_bias)


def solution(mesh):
    in_specs = (
        P("inst", "tm", None),
        P(None, "filt"),
        P("filt", None),
        P(),
        P("inst", "tm", None),
        P("inst"),
        P(None, "tm"),
    )
    out_specs = (P("inst", "tm", None), P(("inst", "tm"), "filt"))
    return jax.shard_map(local, mesh=mesh, in_specs=in_specs, out_specs=out_specs, check_vma=False)
```

```python
import functools

import jax
import jax.numpy as jnp
from jax import lax
from jax.experimental import pallas as pl
from jax.experimental.pallas import tpu as pltpu
from jax.sharding import PartitionSpec as P

f32, bf16, i32, i16 = jnp.float32, jnp.bfloat16, jnp.int32, jnp.int16
MESH = pl.DeviceIdType.MESH
EPOCH = 120
PAD = 16
UNIT = 36
WIDE = 2 * UNIT
WIDE_PAD = 80
SIXTEEN = True


def kernel(
    x, w, cw_hbm, tl_hbm, night_hbm, labels_hbm, bias_hbm,
    logits_hbm, grad_hbm,
    cw, tl, night, labels, bias, logits_out, grad_out,
    xp, wv, y_taps, deriv, pooled, up, xt, grad,
    teach, logit, half_tx, half_rx, total, tx, rx, piece, tx2, rx2,
    small_sem, out_sem, load_sem, halo_send, halo_recv, teach_send, teach_recv, logit_send, logit_recv,
    half_send, half_recv, send1, recv1, send2, recv2,
):
    yy, tm, xx = lax.axis_index("inst"), lax.axis_index("tm"), lax.axis_index("filt")
    zz, cc = tm // 2, tm % 2
    oc = 1 - cc
    ny, nz, nx = 8, 8, 4

    def remote(src, dst, ssem, rsem, dev):
        return pltpu.make_async_remote_copy(
            src_ref=src, dst_ref=dst, send_sem=ssem, recv_sem=rsem, device_id=dev, device_id_type=MESH
        )

    def arrived(dst, rsem):
        remote(dst, dst, rsem, rsem, (yy, tm, xx)).wait_recv()

    barrier = pltpu.get_barrier_semaphore()

    def greet(dev):
        pl.semaphore_signal(barrier, inc=1, device_id=dev, device_id_type=MESH)

    greet((yy, zz * 2 + oc, xx))
    for d in range(1, 8):
        for c in range(2):
            greet((yy, lax.rem(zz + d, nz) * 2 + c, xx))
            greet((lax.rem(yy + d, ny), zz * 2 + c, xx))
    for d in range(1, 4):
        greet((yy, tm, lax.rem(xx + d, nx)))

    pairs = [(tl_hbm, tl), (night_hbm, night), (cw_hbm, cw), (labels_hbm, labels), (bias_hbm, bias)]
    small = [pltpu.make_async_copy(src, dst, small_sem.at[i]) for i, (src, dst) in enumerate(pairs)]
    loads = [pltpu.make_async_copy(w, wv, load_sem.at[4])]
    loads += [
        pltpu.make_async_copy(x.at[i], xp.at[i, pl.ds(PAD, 480)], load_sem.at[i]) for i in range(4)
    ]
    for c in small + loads:
        c.start()

    small[0].wait()
    small[1].wait()
    row = lax.broadcasted_iota(i32, (16, 128), 0)
    lane = lax.broadcasted_iota(i32, (16, 128), 1)
    t5 = jnp.concatenate([tl[i] for i in range(4)], axis=0)
    t5 = jnp.exp(t5 - jnp.max(t5, axis=1, keepdims=True))
    t5 = t5 / jnp.sum(t5, axis=1, keepdims=True)
    tile = jnp.zeros((16, 128), f32)
    for s in range(5):
        tile = jnp.where(lane == s, t5[:, s : s + 1], tile)
    for i in range(4):
        tile = jnp.where((lane == 8) & (row // 4 == i), night[i].astype(f32), tile)
    tile = jnp.where(lane == 9, 1.0, tile)
    teach[yy] = tile

    @pl.when(tm == 0)
    def _():
        for i in range(4):
            xp[i, 0:PAD, :] = jnp.zeros((PAD, 256), bf16)

    @pl.when(tm == 15)
    def _():
        for i in range(4):
            xp[i, PAD + 480 :, :] = jnp.zeros((PAD, 256), bf16)

    def weights(p):
        if p == 4:
            return wv[pl.ds(2048, 256), :]
        return jnp.concatenate([wv[pl.ds(512 * p, 256), :], wv[pl.ds(512 * p + 256, 256), :]], axis=1)

    def forward(i):
        for p in range(5):
            y = jnp.dot(xp[i, PAD : PAD + 480, :], weights(p), preferred_element_type=f32)
            y_taps[i, 2 * p, PAD : PAD + 480, :] = y[:, :128]
            if p < 4:
                y_taps[i, 2 * p + 1, PAD : PAD + 480, :] = y[:, 128:]

    def finish(i, epochs):
        for e in epochs:
            o = PAD - 4 + EPOCH * e
            pre = y_taps[i, 0, pl.ds(o, EPOCH), :]
            for k in range(1, 9):
                pre = pre + y_taps[i, k, pl.ds(o + k, EPOCH), :]
            ex = jnp.exp(jnp.minimum(pre, 0.0))
            act = jnp.where(pre > 0, pre, ex - 1.0)
            deriv[i, pl.ds(EPOCH * e, EPOCH), :] = ex
            pooled[pl.ds(4 * i + e, 1), :] = jnp.sum(act, axis=0, keepdims=True) * (1.0 / EPOCH)

    for c in loads:
        c.wait()
    pl.semaphore_wait(barrier, 32)

    up_halo = remote(
        xp.at[:, pl.ds(480, PAD)], xp.at[:, pl.ds(0, PAD)], halo_send.at[0], halo_recv.at[0], (yy, tm + 1, xx)
    )
    down_halo = remote(
        xp.at[:, pl.ds(PAD, PAD)], xp.at[:, pl.ds(PAD + 480, PAD)], halo_send.at[1], halo_recv.at[1], (yy, tm - 1, xx)
    )
    pl.when(tm < 15)(up_halo.start)
    pl.when(tm > 0)(down_halo.start)
    teach_copies = [
        remote(teach.at[yy], teach.at[yy], teach_send.at[d - 1], teach_recv.at[yy], (lax.rem(yy + d, ny), tm, xx))
        for d in range(1, 8)
    ]
    for c in teach_copies:
        c.start()

    for i in range(4):
        forward(i)
        finish(i, (1, 2))

    pl.when(tm > 0)(up_halo.wait_recv)
    pl.when(tm < 15)(down_halo.wait_recv)
    xh = jnp.concatenate([xp[i, r : r + PAD, :] for i in range(4) for r in (0, PAD + 480)], axis=0)
    for p in range(5):
        y = jnp.dot(xh, weights(p), preferred_element_type=f32)
        for i in range(4):
            for h, r in enumerate((0, PAD + 480)):
                o = (2 * i + h) * PAD
                y_taps[i, 2 * p, r : r + PAD, :] = y[o : o + PAD, :128]
                if p < 4:
                    y_taps[i, 2 * p + 1, r : r + PAD, :] = y[o : o + PAD, 128:]

    for i in range(4):
        finish(i, (0, 3))

    for c in small[2:]:
        c.wait()
    cwt = cw[...]
    pool = pooled[...]
    part = jnp.zeros((16, 128), f32)
    for s in range(5):
        part = jnp.where(lane == s, jnp.sum(pool * cwt[s : s + 1, :], axis=1, keepdims=True), part)
    logit[xx] = part
    logit_copies = [
        remote(logit.at[xx], logit.at[xx], logit_send.at[d - 1], logit_recv.at[xx], (yy, tm, lax.rem(xx + d, nx)))
        for d in range(1, 4)
    ]
    for c in logit_copies:
        c.start()

    for i in range(4):
        xt[:, 512 * i : 512 * i + 512] = xp[i].T
    for d in range(1, 8):
        s = lax.rem(yy + d, ny)
        arrived(teach.at[s], teach_recv.at[s])
    nights = [night[i].astype(f32) for i in range(4)]
    sums = [jnp.zeros((16, 128), f32) for _ in range(4)]
    for j in range(8):
        t = teach[j]
        of = jnp.broadcast_to(t[:, 8:9], (16, 128))
        for i in range(4):
            sums[i] = sums[i] + jnp.where(of == nights[i], t, 0.0)
    soft = []
    for i in range(4):
        s = sums[i][0:4] + sums[i][4:8] + sums[i][8:12] + sums[i][12:16]
        soft.append(s / s[:, 9:10])
    soft = jnp.concatenate(soft, axis=0)
    label = jnp.zeros((16, 128), i32)
    for i in range(4):
        for e in range(4):
            label = jnp.where(row == 4 * i + e, labels[e, night[i]], label)
    target = 0.5 * soft + 0.5 * (lane == label).astype(f32)

    for d in range(1, 4):
        s = lax.rem(xx + d, nx)
        arrived(logit.at[s], logit_recv.at[s])
    logits = logit[0] + logit[1] + logit[2] + logit[3]
    for s in range(5):
        logits = logits + jnp.where(lane == s, bias[s], 0.0)
    for i in range(4):
        logits_out[i] = logits[4 * i : 4 * i + 4, :5]
    logits_copy = pltpu.make_async_copy(logits_out, logits_hbm, out_sem.at[0])
    logits_copy.start()
    expo = jnp.where(lane < 5, jnp.exp(logits), 0.0)
    diff = expo / jnp.sum(expo, axis=1, keepdims=True) - target
    slope = jnp.zeros((16, 128), f32)
    for s in range(5):
        slope = slope + diff[:, s : s + 1] * cwt[s : s + 1, :]

    for i in range(4):
        up[i, 0:24, :] = jnp.zeros((24, 128), f32)
        up[i, 504:528, :] = jnp.zeros((24, 128), f32)
        for e in range(4):
            up[i, pl.ds(24 + EPOCH * e, EPOCH), :] = (
                deriv[i, pl.ds(EPOCH * e, EPOCH), :] * slope[4 * i + e : 4 * i + e + 1, :]
            )
    for p in range(5):
        acc = None
        for i in range(4):
            us = [up[i, pl.ds(12 - k, 512), :].astype(bf16) for k in range(2 * p, min(2 * p + 2, 9))]
            u = jnp.concatenate(us, axis=1) if p < 4 else us[0]
            g = jnp.dot(xt[:, 512 * i : 512 * i + 512], u, preferred_element_type=f32)
            acc = g if acc is None else acc + g
        grad[pl.ds(512 * p, 256), :] = acc[:, :128]
        if p < 4:
            grad[pl.ds(512 * p + 256, 256), :] = acc[:, 128:]

    def rows_of(j, h, core):
        if j < 8:
            return pl.ds(pl.multiple_of(core * 144, 8) + 288 * j + UNIT * (j % 2 + 2 * h), UNIT)
        z = j - 8
        return pl.ds(pl.multiple_of(core * 1152, 8) + 288 * (1 - z % 2 + 2 * h) + UNIT * z, UNIT)

    partner = (yy, zz * 2 + oc, xx)
    half_copies = []
    for part_at in range(2):
        for j in range(8 * part_at, 8 * part_at + 8):
            for h in range(2):
                half_tx[j, UNIT * h : UNIT * h + UNIT, :] = grad[rows_of(j, h, oc), :]
        sl = pl.ds(8 * part_at, 8)
        c = remote(half_tx.at[sl], half_rx.at[sl], half_send.at[part_at], half_recv.at[part_at], partner)
        c.start()
        half_copies.append(c)

    copies1 = []
    for part_at in range(2):
        half_copies[part_at].wait_recv()
        top = jnp.zeros((WIDE, 128), f32)
        for j in range(8 * part_at, 8 * part_at + 8):
            t = half_rx[j] + jnp.concatenate([grad[rows_of(j, h, cc), :] for h in range(2)], axis=0)
            total[j] = t
            top = jnp.maximum(top, jnp.abs(t))
        if SIXTEEN:
            top = jnp.max(top, axis=0, keepdims=True)
            power = jnp.ceil(jnp.log2(jnp.maximum(top, 1e-30)) + 0.01)
            factor = jnp.exp2(15.0 - power)
            power = jnp.broadcast_to(power, (WIDE_PAD - WIDE, 128))
            for j in range(8 * part_at, 8 * part_at + 8):
                q = jnp.concatenate([jnp.round(total[j] * factor), power], axis=0)
                tx[j] = q.astype(i32).astype(i16)
        else:
            for j in range(8 * part_at, 8 * part_at + 8):
                tx[j] = total[j]
        for d in (4, 3, 5, 2, 6, 1, 7):
            if part_at == 0:
                to, me = lax.rem(yy + d, ny), yy
                dev = (to, tm, xx)
            else:
                to, me = lax.rem(zz + d, nz), zz
                dev = (yy, to * 2 + cc, xx)
            base = 8 * part_at
            c = remote(
                tx.at[base + to], rx.at[base + me], send1.at[7 * part_at + d - 1], recv1.at[base + me], dev
            )
            c.start()
            copies1.append(c)

    copies2 = []
    for part_at in range(2):
        base = 8 * part_at
        me = yy if part_at == 0 else zz
        acc = total[base + me]
        for d in (1, 7, 2, 6, 3, 5, 4):
            s = base + lax.rem(me + d, 8)
            arrived(rx.at[s], recv1.at[s])
            t = rx[s].astype(f32)
            if SIXTEEN:
                t = t[:WIDE] * jnp.exp2(t[WIDE : WIDE + 1] - 15.0)
            acc = acc + t
        piece[part_at, 0:WIDE, :] = acc
        piece[part_at, WIDE:, :] = jnp.zeros((WIDE_PAD - WIDE, 128), f32)
        for m in range(4):
            tx2[4 * part_at + m] = piece[part_at, pl.ds(18 * m, 24), :]
        for m in range(4):
            h, c = m // 2, m % 2
            slot = 4 * part_at + m
            if part_at == 0:
                to, own = yy % 2 + 4 * cc + 2 * h, zz
                dev = (yy, to * 2 + c, xx)
                mine = (to == zz) & (cc == c)
            else:
                to, own = 4 * cc + 1 - zz % 2 + 2 * h, yy
                dev = (to, zz * 2 + c, xx)
                mine = (to == yy) & (cc == c)
            copy = remote(tx2.at[slot], rx2.at[own], send2.at[slot], recv2.at[own], dev)
            copies2.append((copy, mine))

            @pl.when(mine)
            def _():
                rx2[own] = tx2[slot]

            @pl.when(jnp.logical_not(mine))
            def _():
                copy.start()

    even = (yy + zz) % 2 == 0
    holder = jnp.where(even, zz // 4, yy // 4)
    place = jnp.where(even, zz, yy)
    for s in range(8):
        @pl.when(jnp.logical_not((place == s) & (holder == cc)))
        def _():
            arrived(rx2.at[s], recv2.at[s])
    out = rx2[0]
    for s in range(1, 8):
        out = out + rx2[s]
    grad_out[...] = out[:18] * (1.0 / 32)
    grad_copy = pltpu.make_async_copy(grad_out, grad_hbm, out_sem.at[1])
    grad_copy.start()

    pl.when(tm < 15)(up_halo.wait_send)
    pl.when(tm > 0)(down_halo.wait_send)
    for c in teach_copies + logit_copies + half_copies + copies1:
        c.wait_send()
    for c, mine in copies2:
        pl.when(jnp.logical_not(mine))(c.wait_send)
    logits_copy.wait()
    grad_copy.wait()


def local(activations, conv_weight, class_weight, class_bias, teacher_logits, night_of, section_labels):
    hbm = pl.BlockSpec(memory_space=pltpu.HBM)
    wire, wire_rows = (i16, WIDE_PAD) if SIXTEEN else (f32, WIDE)
    dma = pltpu.SemaphoreType.DMA
    return pl.pallas_call(
        kernel,
        out_shape=(jax.ShapeDtypeStruct((4, 4, 5), f32), jax.ShapeDtypeStruct((18, 128), f32)),
        in_specs=[hbm] * 7,
        out_specs=(hbm, hbm),
        scratch_shapes=[
            pltpu.VMEM((5, 128), f32),
            pltpu.VMEM((4, 4, 5), f32),
            pltpu.SMEM((4,), i32),
            pltpu.SMEM((4, 8), i32),
            pltpu.SMEM((5,), f32),
            pltpu.VMEM((4, 4, 5), f32),
            pltpu.VMEM((18, 128), f32),
            pltpu.VMEM((4, 512, 256), bf16),
            pltpu.VMEM((2304, 128), bf16),
            pltpu.VMEM((4, 9, 512, 128), f32),
            pltpu.VMEM((4, 480, 128), f32),
            pltpu.VMEM((16, 128), f32),
            pltpu.VMEM((4, 528, 128), f32),
            pltpu.VMEM((256, 2048), bf16),
            pltpu.VMEM((2304, 128), f32),
            pltpu.VMEM((8, 16, 128), f32),
            pltpu.VMEM((4, 16, 128), f32),
            pltpu.VMEM((16, WIDE, 128), f32),
            pltpu.VMEM((16, WIDE, 128), f32),
            pltpu.VMEM((16, WIDE, 128), f32),
            pltpu.VMEM((16, wire_rows, 128), wire),
            pltpu.VMEM((16, wire_rows, 128), wire),
            pltpu.VMEM((2, WIDE_PAD, 128), f32),
            pltpu.VMEM((8, 24, 128), f32),
            pltpu.VMEM((8, 24, 128), f32),
            dma((5,)), dma((2,)), dma((5,)),
            dma((2,)), dma((2,)),
            dma((7,)), dma((8,)),
            dma((3,)), dma((4,)),
            dma((2,)), dma((2,)),
            dma((14,)), dma((16,)),
            dma((8,)), dma((8,)),
        ],
        compiler_params=pltpu.CompilerParams(
            collective_id=0, has_side_effects=True, vmem_limit_bytes=63 << 20
        ),
    )(activations, conv_weight, class_weight.T, teacher_logits, night_of, section_labels.T, class_bias)


def solution(mesh):
    in_specs = (
        P("inst", "tm", None),
        P(None, "filt"),
        P("filt", None),
        P(),
        P("inst", "tm", None),
        P("inst"),
        P(None, "tm"),
    )
    out_specs = (P("inst", "tm", None), P(("inst", "tm"), "filt"))
    return jax.shard_map(local, mesh=mesh, in_specs=in_specs, out_specs=out_specs, check_vma=False)
```

```python
import functools

import jax
import jax.numpy as jnp
from jax import lax
from jax.experimental import pallas as pl
from jax.experimental.pallas import tpu as pltpu
from jax.sharding import PartitionSpec as P

f32, bf16, i32, i16 = jnp.float32, jnp.bfloat16, jnp.int32, jnp.int16
MESH = pl.DeviceIdType.MESH
EPOCH = 120
PAD = 16
UNIT = 36
WIDE = 2 * UNIT
WIDE_PAD = 80
LONG = 1024
TN = False


def kernel(
    x, w, cw_hbm, tl_hbm, night_hbm, labels_hbm, bias_hbm,
    logits_out, grad_out,
    cw, tl, night, labels, bias,
    xc, wv, y_taps, deriv, pooled, up, xt, grad,
    teach, goal, logit, tx, rx, piece, tx2, rx2,
    small_sem, load_sem, halo_send, halo_recv, pair_send, pair_recv,
    teach_send, teach_recv, logit_send, logit_recv, send1, recv1, send2, recv2,
):
    yy, tm, xx = lax.axis_index("inst"), lax.axis_index("tm"), lax.axis_index("filt")
    zz, cc = tm // 2, tm % 2
    oc = 1 - cc
    ny, nz, nx = 8, 8, 4

    def remote(src, dst, ssem, rsem, dev):
        return pltpu.make_async_remote_copy(
            src_ref=src, dst_ref=dst, send_sem=ssem, recv_sem=rsem, device_id=dev, device_id_type=MESH
        )

    def arrived(dst, rsem):
        remote(dst, dst, rsem, rsem, (yy, tm, xx)).wait_recv()

    barrier = pltpu.get_barrier_semaphore()

    def greet(dev):
        pl.semaphore_signal(barrier, inc=1, device_id=dev, device_id_type=MESH)

    greet((yy, zz * 2 + oc, xx))
    for d in range(1, 8):
        for c in range(2):
            greet((yy, lax.rem(zz + d, nz) * 2 + c, xx))
            greet((lax.rem(yy + d, ny), zz * 2 + c, xx))
    for d in range(1, 4):
        for c in range(2):
            greet((yy, zz * 2 + c, lax.rem(xx + d, nx)))

    start = pl.multiple_of(480 * cc, 16)
    own = pl.ds(pl.multiple_of(PAD + 480 * cc, 16), 480)
    pairs = [(tl_hbm, tl), (night_hbm, night), (cw_hbm, cw), (labels_hbm, labels), (bias_hbm, bias)]
    small = [pltpu.make_async_copy(src, dst, small_sem.at[i]) for i, (src, dst) in enumerate(pairs)]
    loads = [pltpu.make_async_copy(w, wv, load_sem.at[4])]
    loads += [
        pltpu.make_async_copy(x.at[i], xc.at[i, own], load_sem.at[i]) for i in range(4)
    ]
    for c in small + loads:
        c.start()

    small[0].wait()
    small[1].wait()
    row = lax.broadcasted_iota(i32, (16, 128), 0)
    lane = lax.broadcasted_iota(i32, (16, 128), 1)
    t5 = jnp.concatenate([tl[i] for i in range(4)], axis=0)
    t5 = jnp.exp(t5 - jnp.max(t5, axis=1, keepdims=True))
    t5 = t5 / jnp.sum(t5, axis=1, keepdims=True)
    tile = jnp.zeros((16, 128), f32)
    for s in range(5):
        tile = jnp.where(lane == s, t5[:, s : s + 1], tile)
    for i in range(4):
        tile = jnp.where((lane == 8) & (row // 4 == i), night[i].astype(f32), tile)
    tile = jnp.where(lane == 9, 1.0, tile)
    teach[yy] = tile[0:8] + pltpu.roll(tile[8:16], 16, 1)

    @pl.when(zz == 0)
    def _():
        for i in range(4):
            xc[i, 0:PAD, :] = jnp.zeros((PAD, 256), bf16)

    @pl.when(zz == nz - 1)
    def _():
        for i in range(4):
            xc[i, PAD + 960 : 2 * PAD + 960, :] = jnp.zeros((PAD, 256), bf16)

    for i in range(4):
        xc[i, 2 * PAD + 960 :, :] = jnp.zeros((LONG - 2 * PAD - 960, 256), bf16)
        up[i, 0:24, :] = jnp.zeros((24, 128), f32)
        up[i, 984:, :] = jnp.zeros((56, 128), f32)

    def weights(p):
        if p == 4:
            return wv[pl.ds(2048, 256), :]
        return jnp.concatenate([wv[pl.ds(512 * p, 256), :], wv[pl.ds(512 * p + 256, 256), :]], axis=1)

    def forward(i):
        for p in range(5):
            y = jnp.dot(xc[i, own, :], weights(p), preferred_element_type=f32)
            y_taps[i, 2 * p, PAD : PAD + 480, :] = y[:, :128]
            if p < 4:
                y_taps[i, 2 * p + 1, PAD : PAD + 480, :] = y[:, 128:]

    def finish(i, epochs):
        for e in epochs:
            o = PAD - 4 + EPOCH * e
            pre = y_taps[i, 0, pl.ds(o, EPOCH), :]
            for k in range(1, 9):
                pre = pre + y_taps[i, k, pl.ds(o + k, EPOCH), :]
            ex = jnp.exp(jnp.minimum(pre, 0.0))
            act = jnp.where(pre > 0, pre, ex - 1.0)
            deriv[i, pl.ds(pl.multiple_of(start + EPOCH * e, 8), EPOCH), :] = ex
            pooled[pl.ds(4 * i + e, 1), :] = jnp.sum(act, axis=0, keepdims=True) * (1.0 / EPOCH)

    for c in loads:
        c.wait()
    pl.semaphore_wait(barrier, 35)

    partner = (yy, zz * 2 + oc, xx)
    pair_copies = []

    def to_partner(ref, rows):
        k = len(pair_copies)
        c = remote(ref.at[:, rows], ref.at[:, rows], pair_send.at[k], pair_recv.at[k], partner)
        c.start()
        pair_copies.append(c)

    halo_src = pl.ds(pl.multiple_of(PAD + 944 * cc, 16), PAD)
    halo_dst = pl.ds(pl.multiple_of((PAD + 960) * oc, 16), PAD)
    has_next = jnp.where(cc == 0, zz > 0, zz < nz - 1)
    halo_copies = [
        remote(
            xc.at[:, halo_src], xc.at[:, halo_dst], halo_send.at[c], halo_recv.at[oc],
            (yy, (zz - 1 + 2 * cc) * 2 + c, xx),
        )
        for c in range(2)
    ]

    @pl.when(has_next)
    def _():
        for c in halo_copies:
            c.start()

    teach_copies = [
        remote(teach.at[yy], teach.at[yy], teach_send.at[d - 1], teach_recv.at[yy], (lax.rem(yy + d, ny), tm, xx))
        for d in (4, 3, 5, 2, 6, 1, 7)
    ]
    for c in teach_copies:
        c.start()
    to_partner(xc, pl.ds(pl.multiple_of(480 + 16 * cc, 16), PAD))

    for i in range(4):
        forward(i)
        finish(i, (1, 2))

    to_partner(xc, pl.ds(pl.multiple_of(PAD + 496 * cc, 16), 464))
    to_partner(deriv, pl.ds(pl.multiple_of(start + EPOCH, 8), 2 * EPOCH))
    pair_copies[0].wait_recv()

    @pl.when(zz > 0)
    def _():
        arrived(xc.at[:, pl.ds(0, PAD)], halo_recv.at[0])

    @pl.when(zz < nz - 1)
    def _():
        arrived(xc.at[:, pl.ds(PAD + 960, PAD)], halo_recv.at[1])

    ends = [pl.ds(start, PAD), pl.ds(pl.multiple_of(start + PAD + 480, 16), PAD)]
    xh = jnp.concatenate([xc[i, r, :] for i in range(4) for r in ends], axis=0)
    for p in range(5):
        y = jnp.dot(xh, weights(p), preferred_element_type=f32)
        for i in range(4):
            for h, r in enumerate((0, PAD + 480)):
                o = (2 * i + h) * PAD
                y_taps[i, 2 * p, r : r + PAD, :] = y[o : o + PAD, :128]
                if p < 4:
                    y_taps[i, 2 * p + 1, r : r + PAD, :] = y[o : o + PAD, 128:]

    for i in range(4):
        finish(i, (0, 3))

    for c in small[2:]:
        c.wait()
    cwt = cw[...]
    pool = pooled[...]
    part = jnp.zeros((8, 128), f32)
    for s in range(5):
        t = jnp.sum(pool * cwt[s : s + 1, :], axis=1, keepdims=True)
        part = jnp.where(lane[0:8] == s, t[0:8], part)
        part = jnp.where(lane[0:8] == 16 + s, t[8:16], part)
    logit[cc, xx] = part
    logit_copies = []
    for d in (2, 1, 3, 0):
        for c in range(2):
            if d:
                dev = (yy, zz * 2 + c, lax.rem(xx + d, nx))
            elif c == 0:
                dev = partner
            else:
                continue
            k = len(logit_copies)
            logit_copies.append(
                remote(logit.at[cc, xx], logit.at[cc, xx], logit_send.at[k], logit_recv.at[cc, xx], dev)
            )
    for c in logit_copies:
        c.start()

    to_partner(deriv, pl.ds(start, EPOCH))
    to_partner(deriv, pl.ds(pl.multiple_of(start + 3 * EPOCH, 8), EPOCH))

    pair_copies[1].wait_recv()
    for i in range(4):
        xt[i] = xc[i].T
    for d in range(1, 8):
        s = lax.rem(yy + d, ny)
        arrived(teach.at[s], teach_recv.at[s])
    nights = [night[i].astype(f32) for i in range(4)]
    lane8 = lane[0:8]
    sums = [jnp.zeros((8, 128), f32) for _ in range(4)]
    for j in range(8):
        t = teach[j]
        of = jnp.where(lane8 < 16, t[:, 8:9], t[:, 24:25])
        for i in range(4):
            sums[i] = sums[i] + jnp.where(of == nights[i], t, 0.0)
    soft = []
    for i in range(4):
        s = sums[i] + pltpu.roll(sums[i], 112, 1)
        s = s[0:4] + s[4:8]
        soft.append(s / s[:, 9:10])
    soft = jnp.concatenate(soft, axis=0)
    label = jnp.zeros((16, 128), i32)
    for i in range(4):
        for e in range(4):
            label = jnp.where(row == 4 * i + e, labels[e, night[i]], label)
    goal[cc] = 0.5 * soft + 0.5 * (lane == label).astype(f32)
    goal_copy = remote(goal.at[cc], goal.at[cc], pair_send.at[5], pair_recv.at[5], partner)
    goal_copy.start()

    for d in range(1, 4):
        s = lax.rem(xx + d, nx)
        for c in range(2):
            arrived(logit.at[c, s], logit_recv.at[c, s])
    arrived(logit.at[oc, xx], logit_recv.at[oc, xx])
    goal_copy.wait_recv()
    shift = jnp.zeros((16, 128), f32)
    for s in range(5):
        shift = shift + jnp.where(lane == s, bias[s], 0.0)
    slopes, both = [], []
    for b in range(2):
        logits = logit[b, 0] + logit[b, 1] + logit[b, 2] + logit[b, 3]
        logits = jnp.concatenate([logits, pltpu.roll(logits, 112, 1)], axis=0) + shift
        both.append(logits)
        expo = jnp.where(lane < 5, jnp.exp(logits), 0.0)
        diff = expo / jnp.sum(expo, axis=1, keepdims=True) - goal[b]
        slope = jnp.zeros((16, 128), f32)
        for s in range(5):
            slope = slope + diff[:, s : s + 1] * cwt[s : s + 1, :]
        slopes.append(slope)
    logits = jnp.where(cc == 0, both[0], both[1])
    for i in range(4):
        logits_out[i] = logits[4 * i : 4 * i + 4, :5]

    for c in pair_copies[2:]:
        c.wait_recv()
    for i in range(4):
        for b in range(2):
            for e in range(4):
                o = 480 * b + EPOCH * e
                up[i, pl.ds(24 + o, EPOCH), :] = (
                    deriv[i, pl.ds(o, EPOCH), :] * slopes[b][4 * i + e : 4 * i + e + 1, :]
                )

    def backward(taps, channels, at):
        acc = None
        for i in range(4):
            us = [up[i, pl.ds(12 - k, LONG), :].astype(bf16) for k in taps]
            u = us[0] if len(us) == 1 else jnp.concatenate(us, axis=1)
            g = jnp.dot(xt[i, channels, :], u, preferred_element_type=f32)
            acc = g if acc is None else acc + g
        for n in range(len(taps)):
            grad[pl.ds(at + acc.shape[0] * n, acc.shape[0]), :] = acc[:, 128 * n : 128 * n + 128]

    @pl.when(cc == 0)
    def _():
        backward((0, 1), slice(None), 0)
        backward((2, 3), slice(None), 512)
        backward((4,), slice(0, 128), 1024)

    @pl.when(cc == 1)
    def _():
        backward((4,), slice(128, 256), 0)
        backward((5, 6), slice(None), 128)
        backward((7, 8), slice(None), 640)

    def rows_of(j, h):
        if j < 8:
            y, z = j // 2, j // 2 % 2 + 4 * (j % 2) + 2 * h
        else:
            y, z = 1 - j % 2 + 2 * h, j - 8
        return pl.ds(288 * y + UNIT * z, UNIT)

    holder1 = yy // 4 == cc
    copies1 = []
    for part_at in range(2):
        base = 8 * part_at
        top = jnp.max(jnp.abs(grad[...]), axis=0, keepdims=True) if part_at == 0 else top
        if part_at == 0:
            power = jnp.ceil(jnp.log2(jnp.maximum(top, 1e-30)) + 0.01)
            factor = jnp.exp2(15.0 - power)
            power = jnp.broadcast_to(power, (WIDE_PAD - WIDE, 128))
        for j in range(base, base + 8):
            t = jnp.concatenate([grad[rows_of(j, h), :] for h in range(2)], axis=0)
            q = jnp.concatenate([jnp.round(t * factor), power], axis=0)
            tx[j] = q.astype(i32).astype(i16)
        if part_at == 0:
            for m, (near, far) in enumerate(((2, 0), (3, 1), (1, 3), (0, 2))):
                j = lax.rem(yy + jnp.where(holder1, near, far), 4)
                for h in range(2):
                    mine = (yy == 4 * cc + j) & (cc == h)
                    c = remote(
                        tx.at[2 * j + h], rx.at[yy], send1.at[2 * m + h], recv1.at[yy], (4 * cc + j, zz * 2 + h, xx)
                    )
                    copies1.append((c, mine))
                    pl.when(jnp.logical_not(mine))(c.start)

            @pl.when(holder1)
            def _():
                rx[yy] = tx[2 * lax.rem(yy, 4) + cc]

        else:
            rx[8 + zz] = tx[8 + zz]
            for d in (4, 3, 5, 2, 6, 1, 7):
                to = lax.rem(zz + d, nz)
                c = remote(
                    tx.at[8 + to], rx.at[8 + zz], send1.at[8 + d], recv1.at[8 + zz], (yy, to * 2 + cc, xx)
                )
                c.start()
                copies1.append((c, None))

    copies2 = []
    for part_at in range(2):
        base = 8 * part_at
        me = yy if part_at == 0 else zz
        if part_at == 0:
            for s in range(8):
                @pl.when(jnp.logical_not(holder1 & (yy == s)))
                def _():
                    arrived(rx.at[s], recv1.at[s])
        else:
            for d in (1, 7, 2, 6, 3, 5, 4):
                s = base + lax.rem(me + d, 8)
                arrived(rx.at[s], recv1.at[s])
        acc = jnp.zeros((WIDE, 128), f32)
        for s in range(base, base + 8):
            t = rx[s].astype(f32)
            acc = acc + t[:WIDE] * jnp.exp2(t[WIDE : WIDE + 1] - 15.0)
        piece[part_at, 0:WIDE, :] = acc
        piece[part_at, WIDE:, :] = jnp.zeros((WIDE_PAD - WIDE, 128), f32)
        for m in range(4):
            tx2[4 * part_at + m] = piece[part_at, pl.ds(18 * m, 24), :]
        for m in range(4):
            h, c = m // 2, m % 2
            slot = 4 * part_at + m
            if part_at == 0:
                to, own = yy % 2 + 4 * cc + 2 * h, zz
                dev = (yy, to * 2 + c, xx)
                mine = (to == zz) & (cc == c)
            else:
                to, own = 4 * cc + 1 - zz % 2 + 2 * h, yy
                dev = (to, zz * 2 + c, xx)
                mine = (to == yy) & (cc == c)
            copy = remote(tx2.at[slot], rx2.at[own], send2.at[slot], recv2.at[own], dev)
            copies2.append((copy, mine))

            @pl.when(mine)
            def _():
                rx2[own] = tx2[slot]

            @pl.when(jnp.logical_not(mine))
            def _():
                copy.start()

    even = (yy + zz) % 2 == 0
    holder = jnp.where(even, zz // 4, yy // 4)
    place = jnp.where(even, zz, yy)
    for s in range(8):
        @pl.when(jnp.logical_not((place == s) & (holder == cc)))
        def _():
            arrived(rx2.at[s], recv2.at[s])
    out = rx2[0]
    for s in range(1, 8):
        out = out + rx2[s]
    grad_out[...] = out[:18] * (1.0 / 32)

    @pl.when(has_next)
    def _():
        for c in halo_copies:
            c.wait_send()

    for c in pair_copies + [goal_copy] + teach_copies + logit_copies:
        c.wait_send()
    for c, mine in copies1 + copies2:
        if mine is None:
            c.wait_send()
        else:
            pl.when(jnp.logical_not(mine))(c.wait_send)


def local(activations, conv_weight, class_weight, class_bias, teacher_logits, night_of, section_labels):
    hbm = pl.BlockSpec(memory_space=pltpu.HBM)
    vm = pl.BlockSpec(memory_space=pltpu.VMEM)
    dma = pltpu.SemaphoreType.DMA
    return pl.pallas_call(
        kernel,
        out_shape=(pltpu.VMEM((4, 4, 5), f32), pltpu.VMEM((18, 128), f32)),
        in_specs=[hbm] * 7,
        out_specs=(vm, vm),
        scratch_shapes=[
            pltpu.VMEM((5, 128), f32),
            pltpu.VMEM((4, 4, 5), f32),
            pltpu.SMEM((4,), i32),
            pltpu.SMEM((4, 8), i32),
            pltpu.SMEM((5,), f32),
            pltpu.VMEM((4, LONG, 256), bf16),
            pltpu.VMEM((2304, 128), bf16),
            pltpu.VMEM((4, 9, 512, 128), f32),
            pltpu.VMEM((4, 960, 128), f32),
            pltpu.VMEM((16, 128), f32),
            pltpu.VMEM((4, LONG + 16, 128), f32),
            pltpu.VMEM((4, 256, LONG), bf16),
            pltpu.VMEM((1152, 128), f32),
            pltpu.VMEM((8, 8, 128), f32),
            pltpu.VMEM((2, 16, 128), f32),
            pltpu.VMEM((2, 4, 8, 128), f32),
            pltpu.VMEM((16, WIDE_PAD, 128), i16),
            pltpu.VMEM((16, WIDE_PAD, 128), i16),
            pltpu.VMEM((2, WIDE_PAD, 128), f32),
            pltpu.VMEM((8, 24, 128), f32),
            pltpu.VMEM((8, 24, 128), f32),
            dma((5,)), dma((5,)),
            dma((2,)), dma((2,)),
            dma((6,)), dma((6,)),
            dma((7,)), dma((8,)),
            dma((7,)), dma((2, 4)),
            dma((16,)), dma((16,)),
            dma((8,)), dma((8,)),
        ],
        compiler_params=pltpu.CompilerParams(
            collective_id=0, has_side_effects=True, vmem_limit_bytes=63 << 20
        ),
    )(activations, conv_weight, class_weight.T, teacher_logits, night_of, section_labels.T, class_bias)


def solution(mesh):
    in_specs = (
        P("inst", "tm", None),
        P(None, "filt"),
        P("filt", None),
        P(),
        P("inst", "tm", None),
        P("inst"),
        P(None, "tm"),
    )
    out_specs = (P("inst", "tm", None), P(("inst", "tm"), "filt"))
    return jax.shard_map(local, mesh=mesh, in_specs=in_specs, out_specs=out_specs, check_vma=False)
```

```python
import functools

import jax
import jax.numpy as jnp
from jax import lax
from jax.experimental import pallas as pl
from jax.experimental.pallas import tpu as pltpu
from jax.sharding import PartitionSpec as P

f32, bf16, i32, i16 = jnp.float32, jnp.bfloat16, jnp.int32, jnp.int16
MESH = pl.DeviceIdType.MESH
EPOCH = 120
PAD = 16
UNIT = 36
WIDE = 2 * UNIT
LONG = 1024
TN = False


def kernel(
    x, w, cw_hbm, tl_hbm, night_hbm, labels_hbm, bias_hbm,
    logits_out, grad_out,
    cw, tl, night, labels, bias,
    xc, wv, y_taps, deriv, pooled, up, xt, grad,
    teach, goal, logit, tx, rx, piece, tx2, rx2,
    small_sem, load_sem, halo_send, halo_recv, pair_send, pair_recv,
    teach_send, teach_recv, logit_send, logit_recv, send1, recv1, send2, recv2,
):
    yy, tm, xx = lax.axis_index("inst"), lax.axis_index("tm"), lax.axis_index("filt")
    zz, cc = tm // 2, tm % 2
    oc = 1 - cc
    ny, nz, nx = 8, 8, 4

    def remote(src, dst, ssem, rsem, dev):
        return pltpu.make_async_remote_copy(
            src_ref=src, dst_ref=dst, send_sem=ssem, recv_sem=rsem, device_id=dev, device_id_type=MESH
        )

    def arrived(dst, rsem):
        remote(dst, dst, rsem, rsem, (yy, tm, xx)).wait_recv()

    barrier = pltpu.get_barrier_semaphore()

    def greet(dev):
        pl.semaphore_signal(barrier, inc=1, device_id=dev, device_id_type=MESH)

    def greet_z(d):
        for c in range(2):
            greet((yy, lax.rem(zz + d, nz) * 2 + c, xx))

    def greet_y(d):
        for c in range(2):
            greet((lax.rem(yy + d, ny), zz * 2 + c, xx))

    greet_z(7)
    greet_z(1)
    greet((yy, zz * 2 + oc, xx))
    for d in range(1, 4):
        for c in range(2):
            greet((yy, zz * 2 + c, lax.rem(xx + d, nx)))
    for d in (1, 7, 2, 6, 3, 5, 4):
        greet_y(d)
    for d in (6, 2, 5, 3, 4):
        greet_z(d)

    start = pl.multiple_of(480 * cc, 16)
    own = pl.ds(pl.multiple_of(PAD + 480 * cc, 16), 480)
    pairs = [(tl_hbm, tl), (night_hbm, night), (cw_hbm, cw), (labels_hbm, labels), (bias_hbm, bias)]
    small = [pltpu.make_async_copy(src, dst, small_sem.at[i]) for i, (src, dst) in enumerate(pairs)]
    loads = [pltpu.make_async_copy(w, wv, load_sem.at[4])]
    loads += [
        pltpu.make_async_copy(x.at[i], xc.at[i, own], load_sem.at[i]) for i in range(4)
    ]
    for c in small + loads:
        c.start()

    small[0].wait()
    small[1].wait()
    row = lax.broadcasted_iota(i32, (16, 128), 0)
    lane = lax.broadcasted_iota(i32, (16, 128), 1)
    t5 = jnp.concatenate([tl[i] for i in range(4)], axis=0)
    t5 = jnp.exp(t5 - jnp.max(t5, axis=1, keepdims=True))
    t5 = t5 / jnp.sum(t5, axis=1, keepdims=True)
    tile = jnp.zeros((16, 128), f32)
    for s in range(5):
        tile = jnp.where(lane == s, t5[:, s : s + 1], tile)
    for i in range(4):
        tile = jnp.where((lane == 8) & (row // 4 == i), night[i].astype(f32), tile)
    tile = jnp.where(lane == 9, 1.0, tile)
    teach[yy] = tile[0:8] + pltpu.roll(tile[8:16], 16, 1)

    @pl.when(zz == 0)
    def _():
        for i in range(4):
            xc[i, 0:PAD, :] = jnp.zeros((PAD, 256), bf16)

    @pl.when(zz == nz - 1)
    def _():
        for i in range(4):
            xc[i, PAD + 960 : 2 * PAD + 960, :] = jnp.zeros((PAD, 256), bf16)

    for i in range(4):
        xc[i, 2 * PAD + 960 :, :] = jnp.zeros((LONG - 2 * PAD - 960, 256), bf16)
        up[i, 0:24, :] = jnp.zeros((24, 128), f32)
        up[i, 984:, :] = jnp.zeros((56, 128), f32)

    def weights(p):
        if p == 4:
            return wv[pl.ds(2048, 256), :]
        return jnp.concatenate([wv[pl.ds(512 * p, 256), :], wv[pl.ds(512 * p + 256, 256), :]], axis=1)

    def forward(i):
        for p in range(5):
            y = jnp.dot(xc[i, own, :], weights(p), preferred_element_type=f32)
            y_taps[i, 2 * p, PAD : PAD + 480, :] = y[:, :128]
            if p < 4:
                y_taps[i, 2 * p + 1, PAD : PAD + 480, :] = y[:, 128:]

    def finish(i, epochs):
        for e in epochs:
            o = PAD - 4 + EPOCH * e
            pre = y_taps[i, 0, pl.ds(o, EPOCH), :]
            for k in range(1, 9):
                pre = pre + y_taps[i, k, pl.ds(o + k, EPOCH), :]
            ex = jnp.exp(jnp.minimum(pre, 0.0))
            act = jnp.where(pre > 0, pre, ex - 1.0)
            deriv[i, pl.ds(pl.multiple_of(start + EPOCH * e, 8), EPOCH), :] = ex
            pooled[pl.ds(4 * i + e, 1), :] = jnp.sum(act, axis=0, keepdims=True) * (1.0 / EPOCH)

    for c in loads:
        c.wait()
    pl.semaphore_wait(barrier, 35)

    partner = (yy, zz * 2 + oc, xx)
    pair_copies = []

    def to_partner(ref, rows):
        k = len(pair_copies)
        c = remote(ref.at[:, rows], ref.at[:, rows], pair_send.at[k], pair_recv.at[k], partner)
        c.start()
        pair_copies.append(c)

    halo_src = pl.ds(pl.multiple_of(PAD + 944 * cc, 16), PAD)
    halo_dst = pl.ds(pl.multiple_of((PAD + 960) * oc, 16), PAD)
    has_next = jnp.where(cc == 0, zz > 0, zz < nz - 1)
    halo_copies = [
        remote(
            xc.at[:, halo_src], xc.at[:, halo_dst], halo_send.at[c], halo_recv.at[oc],
            (yy, (zz - 1 + 2 * cc) * 2 + c, xx),
        )
        for c in range(2)
    ]

    @pl.when(has_next)
    def _():
        for c in halo_copies:
            c.start()

    nearby = (2, 6, 1, 7)
    teach_copies = [
        remote(teach.at[yy], teach.at[yy], teach_send.at[k], teach_recv.at[yy], (lax.rem(yy + d, ny), tm, xx))
        for k, d in enumerate(nearby)
    ]
    for c in teach_copies:
        c.start()
    to_partner(xc, pl.ds(pl.multiple_of(480 + 16 * cc, 16), PAD))

    for i in range(4):
        forward(i)
        finish(i, (1, 2))

    to_partner(xc, pl.ds(pl.multiple_of(PAD + 496 * cc, 16), 464))
    to_partner(deriv, pl.ds(pl.multiple_of(start + EPOCH, 8), 2 * EPOCH))
    pair_copies[0].wait_recv()

    @pl.when(zz > 0)
    def _():
        arrived(xc.at[:, pl.ds(0, PAD)], halo_recv.at[0])

    @pl.when(zz < nz - 1)
    def _():
        arrived(xc.at[:, pl.ds(PAD + 960, PAD)], halo_recv.at[1])

    ends = [pl.ds(start, PAD), pl.ds(pl.multiple_of(start + PAD + 480, 16), PAD)]
    xh = jnp.concatenate([xc[i, r, :] for i in range(4) for r in ends], axis=0)
    for p in range(5):
        y = jnp.dot(xh, weights(p), preferred_element_type=f32)
        for i in range(4):
            for h, r in enumerate((0, PAD + 480)):
                o = (2 * i + h) * PAD
                y_taps[i, 2 * p, r : r + PAD, :] = y[o : o + PAD, :128]
                if p < 4:
                    y_taps[i, 2 * p + 1, r : r + PAD, :] = y[o : o + PAD, 128:]

    for i in range(4):
        finish(i, (0, 3))

    for c in small[2:]:
        c.wait()
    cwt = cw[...]
    pool = pooled[...]
    part = jnp.zeros((8, 128), f32)
    for s in range(5):
        t = jnp.sum(pool * cwt[s : s + 1, :], axis=1, keepdims=True)
        part = jnp.where(lane[0:8] == s, t[0:8], part)
        part = jnp.where(lane[0:8] == 16 + s, t[8:16], part)
    logit[cc, xx] = part
    logit_copies = []
    for d in (2, 1, 3, 0):
        for c in range(2):
            if d:
                dev = (yy, zz * 2 + c, lax.rem(xx + d, nx))
            elif c == 0:
                dev = partner
            else:
                continue
            k = len(logit_copies)
            logit_copies.append(
                remote(logit.at[cc, xx], logit.at[cc, xx], logit_send.at[k], logit_recv.at[cc, xx], dev)
            )
    for c in logit_copies:
        c.start()

    to_partner(deriv, pl.ds(start, EPOCH))
    to_partner(deriv, pl.ds(pl.multiple_of(start + 3 * EPOCH, 8), EPOCH))

    pair_copies[1].wait_recv()
    for i in range(4):
        xt[i] = xc[i].T
    for d in nearby:
        s = lax.rem(yy + d, ny)
        arrived(teach.at[s], teach_recv.at[s])
    nights = [night[i].astype(f32) for i in range(4)]
    lane8 = lane[0:8]
    sums = [jnp.zeros((8, 128), f32) for _ in range(4)]
    for d in (0, *nearby):
        t = teach[lax.rem(yy + d, ny)]
        of = jnp.where(lane8 < 16, t[:, 8:9], t[:, 24:25])
        for i in range(4):
            sums[i] = sums[i] + jnp.where(of == nights[i], t, 0.0)
    soft = []
    for i in range(4):
        s = sums[i] + pltpu.roll(sums[i], 112, 1)
        s = s[0:4] + s[4:8]
        soft.append(s / s[:, 9:10])
    soft = jnp.concatenate(soft, axis=0)
    label = jnp.zeros((16, 128), i32)
    for i in range(4):
        for e in range(4):
            label = jnp.where(row == 4 * i + e, labels[e, night[i]], label)
    goal[cc] = 0.5 * soft + 0.5 * (lane == label).astype(f32)
    goal_copy = remote(goal.at[cc], goal.at[cc], pair_send.at[5], pair_recv.at[5], partner)
    goal_copy.start()

    for d in range(1, 4):
        s = lax.rem(xx + d, nx)
        for c in range(2):
            arrived(logit.at[c, s], logit_recv.at[c, s])
    arrived(logit.at[oc, xx], logit_recv.at[oc, xx])
    goal_copy.wait_recv()
    shift = jnp.zeros((16, 128), f32)
    for s in range(5):
        shift = shift + jnp.where(lane == s, bias[s], 0.0)
    slopes, both = [], []
    for b in range(2):
        logits = logit[b, 0] + logit[b, 1] + logit[b, 2] + logit[b, 3]
        logits = jnp.concatenate([logits, pltpu.roll(logits, 112, 1)], axis=0) + shift
        both.append(logits)
        expo = jnp.where(lane < 5, jnp.exp(logits), 0.0)
        diff = expo / jnp.sum(expo, axis=1, keepdims=True) - goal[b]
        slope = jnp.zeros((16, 128), f32)
        for s in range(5):
            slope = slope + diff[:, s : s + 1] * cwt[s : s + 1, :]
        slopes.append(slope)
    logits = jnp.where(cc == 0, both[0], both[1])
    for i in range(4):
        logits_out[i] = logits[4 * i : 4 * i + 4, :5]

    for c in pair_copies[2:]:
        c.wait_recv()
    for i in range(4):
        for b in range(2):
            for e in range(4):
                o = 480 * b + EPOCH * e
                up[i, pl.ds(24 + o, EPOCH), :] = (
                    deriv[i, pl.ds(o, EPOCH), :] * slopes[b][4 * i + e : 4 * i + e + 1, :]
                )

    def backward(taps, channels, at):
        acc = None
        for i in range(4):
            us = [up[i, pl.ds(12 - k, LONG), :].astype(bf16) for k in taps]
            u = us[0] if len(us) == 1 else jnp.concatenate(us, axis=1)
            g = jnp.dot(xt[i, channels, :], u, preferred_element_type=f32)
            acc = g if acc is None else acc + g
        for n in range(len(taps)):
            grad[pl.ds(at + acc.shape[0] * n, acc.shape[0]), :] = acc[:, 128 * n : 128 * n + 128]

    @pl.when(cc == 0)
    def _():
        backward((0, 1), slice(None), 0)
        backward((2, 3), slice(None), 512)
        backward((4,), slice(0, 128), 1024)

    @pl.when(cc == 1)
    def _():
        backward((4,), slice(128, 256), 0)
        backward((5, 6), slice(None), 128)
        backward((7, 8), slice(None), 640)

    power = jnp.ceil(jnp.log2(jnp.maximum(jnp.max(jnp.abs(grad[...]), axis=0, keepdims=True), 1e-30)) + 0.01)
    factor = jnp.exp2(15.0 - power)
    power = jnp.broadcast_to(power, (8, 128))

    def code(slot, units):
        t = jnp.concatenate([grad[pl.ds(288 * y + UNIT * z, UNIT), :] for y, z in units], axis=0)
        tx[slot] = jnp.concatenate([jnp.round(t * factor), power], axis=0).astype(i32).astype(i16)

    half_y, half_z = yy // 4 == cc, zz // 4
    copies = []

    def send(copy, sent):
        copies.append((copy, sent))
        pl.when(sent)(copy.start)

    far_first = ((2, 0), (3, 1), (1, 3), (0, 2))
    for h in range(2):
        for j in range(4):
            code(2 * j + h, [(j, j % 2 + 4 * h), (j, j % 2 + 4 * h + 2)])
        for m, (near, far) in enumerate(far_first):
            j = lax.rem(yy + jnp.where(half_y, near, far), 4)
            dev = (4 * cc + j, zz * 2 + h, xx)
            send(
                remote(tx.at[2 * j + h], rx.at[yy], send1.at[4 * h + m], recv1.at[yy], dev),
                jnp.logical_not((yy == 4 * cc + j) & (cc == h)),
            )
        for z in range(4 * h, 4 * h + 4):
            code(8 + z, [(1 - z % 2, z), (3 - z % 2, z)])
        for m, (near, far) in enumerate(far_first):
            z = 4 * h + lax.rem(zz + jnp.where(half_z == h, near, far), 4)
            dev = (yy, z * 2 + cc, xx)
            send(
                remote(tx.at[8 + z], rx.at[8 + zz], send1.at[8 + 4 * h + m], recv1.at[8 + zz], dev),
                zz != z,
            )

    @pl.when(half_y)
    def _():
        rx[yy] = tx[2 * lax.rem(yy, 4) + cc]

    rx[8 + zz] = tx[8 + zz]

    handed = []
    for k in range(2):
        for m in range(4):
            if k == 0:
                own, dev = zz, (yy, (yy % 2 + 4 * cc + 2 * (m // 2)) * 2 + m % 2, xx)
            else:
                own, dev = yy, (4 * cc + 1 - zz % 2 + 2 * (m // 2), zz * 2 + m % 2, xx)
            slot = 4 * k + m
            copy = remote(tx2.at[slot], rx2.at[own], send2.at[slot], recv2.at[own], dev)
            handed.append((copy, (dev[0] != yy) | (dev[1] != tm), own))

    def hand_out(k):
        acc = jnp.zeros((WIDE, 128), f32)
        for s in range(8):
            if k == 0:
                @pl.when(jnp.logical_not(half_y & (yy == s)))
                def _():
                    arrived(rx.at[s], recv1.at[s])
            else:
                @pl.when(zz != s)
                def _():
                    arrived(rx.at[8 + s], recv1.at[8 + s])
        for s in range(8 * k, 8 * k + 8):
            t = rx[s].astype(f32)
            acc = acc + t[:WIDE] * jnp.exp2(t[WIDE : WIDE + 1] - 15.0)
        piece[0:WIDE, :] = acc
        piece[WIDE:, :] = jnp.zeros((8, 128), f32)
        for slot in range(4 * k, 4 * k + 4):
            copy, sent, own = handed[slot]
            tx2[slot] = piece[pl.ds(18 * (slot % 4), 24), :]
            pl.when(sent)(copy.start)

            @pl.when(jnp.logical_not(sent))
            def _():
                rx2[own] = tx2[slot]

    @pl.when(cc == 0)
    def _():
        hand_out(0)
        hand_out(1)

    @pl.when(cc == 1)
    def _():
        hand_out(1)
        hand_out(0)

    copies += [(copy, sent) for copy, sent, _ in handed]
    even = (yy + zz) % 2 == 0
    holder = jnp.where(even, half_z, yy // 4)
    place = jnp.where(even, zz, yy)
    for s in range(8):
        @pl.when(jnp.logical_not((place == s) & (holder == cc)))
        def _():
            arrived(rx2.at[s], recv2.at[s])
    out = rx2[0]
    for s in range(1, 8):
        out = out + rx2[s]
    grad_out[...] = out[:18] * (1.0 / 32)

    @pl.when(has_next)
    def _():
        for c in halo_copies:
            c.wait_send()

    for c in pair_copies + [goal_copy] + teach_copies + logit_copies:
        c.wait_send()
    for c, sent in copies:
        pl.when(sent)(c.wait_send)


def local(activations, conv_weight, class_weight, class_bias, teacher_logits, night_of, section_labels):
    hbm = pl.BlockSpec(memory_space=pltpu.HBM)
    vm = pl.BlockSpec(memory_space=pltpu.VMEM)
    dma = pltpu.SemaphoreType.DMA
    return pl.pallas_call(
        kernel,
        out_shape=(pltpu.VMEM((4, 4, 5), f32), pltpu.VMEM((18, 128), f32)),
        in_specs=[hbm] * 7,
        out_specs=(vm, vm),
        scratch_shapes=[
            pltpu.VMEM((5, 128), f32),
            pltpu.VMEM((4, 4, 5), f32),
            pltpu.SMEM((4,), i32),
            pltpu.SMEM((4, 8), i32),
            pltpu.SMEM((5,), f32),
            pltpu.VMEM((4, LONG, 256), bf16),
            pltpu.VMEM((2304, 128), bf16),
            pltpu.VMEM((4, 9, 512, 128), f32),
            pltpu.VMEM((4, 960, 128), f32),
            pltpu.VMEM((16, 128), f32),
            pltpu.VMEM((4, LONG + 16, 128), f32),
            pltpu.VMEM((4, 256, LONG), bf16),
            pltpu.VMEM((1152, 128), f32),
            pltpu.VMEM((8, 8, 128), f32),
            pltpu.VMEM((2, 16, 128), f32),
            pltpu.VMEM((2, 4, 8, 128), f32),
            pltpu.VMEM((16, WIDE + 8, 128), i16),
            pltpu.VMEM((16, WIDE + 8, 128), i16),
            pltpu.VMEM((WIDE + 8, 128), f32),
            pltpu.VMEM((8, 24, 128), f32),
            pltpu.VMEM((8, 24, 128), f32),
            dma((5,)), dma((5,)),
            dma((2,)), dma((2,)),
            dma((6,)), dma((6,)),
            dma((4,)), dma((8,)),
            dma((7,)), dma((2, 4)),
            dma((16,)), dma((16,)),
            dma((8,)), dma((8,)),
        ],
        compiler_params=pltpu.CompilerParams(
            collective_id=0, has_side_effects=True, vmem_limit_bytes=63 << 20
        ),
    )(activations, conv_weight, class_weight.T, teacher_logits, night_of, section_labels.T, class_bias)


def solution(mesh):
    in_specs = (
        P("inst", "tm", None),
        P(None, "filt"),
        P("filt", None),
        P(),
        P("inst", "tm", None),
        P("inst"),
        P(None, "tm"),
    )
    out_specs = (P("inst", "tm", None), P(("inst", "tm"), "filt"))
    return jax.shard_map(local, mesh=mesh, in_specs=in_specs, out_specs=out_specs, check_vma=False)
```

```python
import functools

import jax
import jax.numpy as jnp
from jax import lax
from jax.experimental import pallas as pl
from jax.experimental.pallas import tpu as pltpu
from jax.sharding import PartitionSpec as P

f32, bf16, i32, i16 = jnp.float32, jnp.bfloat16, jnp.int32, jnp.int16
MESH = pl.DeviceIdType.MESH
EPOCH = 120
PAD = 16
UNIT = 36
WIDE = 2 * UNIT
LONG = 1024
TN = False


def kernel(
    x, w, cw_hbm, tl_hbm, night_hbm, labels_hbm, bias_hbm,
    logits_out, grad_out,
    cw, tl, night, labels, bias,
    xc, wv, y_taps, deriv, pooled, up, xt, grad,
    teach, goal, logit, tx, rx, piece, tx2, rx2,
    small_sem, load_sem, halo_send, halo_recv, pair_send, pair_recv,
    teach_send, teach_recv, logit_send, logit_recv, send1, recv1, send2, recv2, known1, known2,
):
    yy, tm, xx = lax.axis_index("inst"), lax.axis_index("tm"), lax.axis_index("filt")
    zz, cc = tm // 2, tm % 2
    oc = 1 - cc
    ny, nz, nx = 8, 8, 4

    def remote(src, dst, ssem, rsem, dev):
        return pltpu.make_async_remote_copy(
            src_ref=src, dst_ref=dst, send_sem=ssem, recv_sem=rsem, device_id=dev, device_id_type=MESH
        )

    def arrived(dst, rsem):
        remote(dst, dst, rsem, rsem, (yy, tm, xx)).wait_recv()

    barrier = pltpu.get_barrier_semaphore()

    def greet(dev):
        pl.semaphore_signal(barrier, inc=1, device_id=dev, device_id_type=MESH)

    def greet_z(d):
        for c in range(2):
            greet((yy, lax.rem(zz + d, nz) * 2 + c, xx))

    def greet_y(d):
        for c in range(2):
            greet((lax.rem(yy + d, ny), zz * 2 + c, xx))

    greet_z(7)
    greet_z(1)
    greet((yy, zz * 2 + oc, xx))
    for d in range(1, 4):
        for c in range(2):
            greet((yy, zz * 2 + c, lax.rem(xx + d, nx)))
    for d in (1, 7, 2, 6):
        greet_y(d)

    start = pl.multiple_of(480 * cc, 16)
    own = pl.ds(pl.multiple_of(PAD + 480 * cc, 16), 480)
    pairs = [(tl_hbm, tl), (night_hbm, night), (cw_hbm, cw), (labels_hbm, labels), (bias_hbm, bias)]
    small = [pltpu.make_async_copy(src, dst, small_sem.at[i]) for i, (src, dst) in enumerate(pairs)]
    loads = [pltpu.make_async_copy(w, wv, load_sem.at[4])]
    loads += [
        pltpu.make_async_copy(x.at[i], xc.at[i, own], load_sem.at[i]) for i in range(4)
    ]
    for c in small + loads:
        c.start()

    small[0].wait()
    small[1].wait()
    row = lax.broadcasted_iota(i32, (16, 128), 0)
    lane = lax.broadcasted_iota(i32, (16, 128), 1)
    t5 = jnp.concatenate([tl[i] for i in range(4)], axis=0)
    t5 = jnp.exp(t5 - jnp.max(t5, axis=1, keepdims=True))
    t5 = t5 / jnp.sum(t5, axis=1, keepdims=True)
    tile = jnp.zeros((16, 128), f32)
    for s in range(5):
        tile = jnp.where(lane == s, t5[:, s : s + 1], tile)
    for i in range(4):
        tile = jnp.where((lane == 8) & (row // 4 == i), night[i].astype(f32), tile)
    tile = jnp.where(lane == 9, 1.0, tile)
    teach[yy] = tile[0:8] + pltpu.roll(tile[8:16], 16, 1)

    @pl.when(zz == 0)
    def _():
        for i in range(4):
            xc[i, 0:PAD, :] = jnp.zeros((PAD, 256), bf16)

    @pl.when(zz == nz - 1)
    def _():
        for i in range(4):
            xc[i, PAD + 960 : 2 * PAD + 960, :] = jnp.zeros((PAD, 256), bf16)

    for i in range(4):
        xc[i, 2 * PAD + 960 :, :] = jnp.zeros((LONG - 2 * PAD - 960, 256), bf16)
        up[i, 0:24, :] = jnp.zeros((24, 128), f32)
        up[i, 984:, :] = jnp.zeros((56, 128), f32)

    def weights(p):
        if p == 4:
            return wv[pl.ds(2048, 256), :]
        return jnp.concatenate([wv[pl.ds(512 * p, 256), :], wv[pl.ds(512 * p + 256, 256), :]], axis=1)

    def forward(i):
        for p in range(5):
            y = jnp.dot(xc[i, own, :], weights(p), preferred_element_type=f32)
            y_taps[i, 2 * p, PAD : PAD + 480, :] = y[:, :128]
            if p < 4:
                y_taps[i, 2 * p + 1, PAD : PAD + 480, :] = y[:, 128:]

    def finish(i, epochs):
        for e in epochs:
            o = PAD - 4 + EPOCH * e
            pre = y_taps[i, 0, pl.ds(o, EPOCH), :]
            for k in range(1, 9):
                pre = pre + y_taps[i, k, pl.ds(o + k, EPOCH), :]
            ex = jnp.exp(jnp.minimum(pre, 0.0))
            act = jnp.where(pre > 0, pre, ex - 1.0)
            deriv[i, pl.ds(pl.multiple_of(start + EPOCH * e, 8), EPOCH), :] = ex
            pooled[pl.ds(4 * i + e, 1), :] = jnp.sum(act, axis=0, keepdims=True) * (1.0 / EPOCH)

    for c in loads:
        c.wait()
    pl.semaphore_wait(barrier, 19)

    def tell(sem, dev):
        pl.semaphore_signal(sem, inc=1, device_id=dev, device_id_type=MESH)

    def along_y(d):
        return (lax.rem(yy + d, ny), tm, xx)

    def along_z(d):
        return (yy, lax.rem(zz + d, nz) * 2 + cc, xx)

    partner = (yy, zz * 2 + oc, xx)
    pair_copies = []

    def to_partner(ref, rows):
        k = len(pair_copies)
        c = remote(ref.at[:, rows], ref.at[:, rows], pair_send.at[k], pair_recv.at[k], partner)
        c.start()
        pair_copies.append(c)

    halo_src = pl.ds(pl.multiple_of(PAD + 944 * cc, 16), PAD)
    halo_dst = pl.ds(pl.multiple_of((PAD + 960) * oc, 16), PAD)
    has_next = jnp.where(cc == 0, zz > 0, zz < nz - 1)
    halo_copies = [
        remote(
            xc.at[:, halo_src], xc.at[:, halo_dst], halo_send.at[c], halo_recv.at[oc],
            (yy, (zz - 1 + 2 * cc) * 2 + c, xx),
        )
        for c in range(2)
    ]

    @pl.when(has_next)
    def _():
        for c in halo_copies:
            c.start()

    nearby = (2, 6, 1, 7)
    teach_copies = [
        remote(teach.at[yy], teach.at[yy], teach_send.at[k], teach_recv.at[yy], (lax.rem(yy + d, ny), tm, xx))
        for k, d in enumerate(nearby)
    ]
    for c in teach_copies:
        c.start()
    to_partner(xc, pl.ds(pl.multiple_of(480 + 16 * cc, 16), PAD))
    for dev in (along_z(7), along_z(1), along_y(2), along_y(6)):
        tell(known1, dev)

    for i in range(4):
        forward(i)
        finish(i, (1, 2))

    to_partner(xc, pl.ds(pl.multiple_of(PAD + 496 * cc, 16), 464))
    to_partner(deriv, pl.ds(pl.multiple_of(start + EPOCH, 8), 2 * EPOCH))
    pair_copies[0].wait_recv()

    @pl.when(zz > 0)
    def _():
        arrived(xc.at[:, pl.ds(0, PAD)], halo_recv.at[0])

    @pl.when(zz < nz - 1)
    def _():
        arrived(xc.at[:, pl.ds(PAD + 960, PAD)], halo_recv.at[1])

    ends = [pl.ds(start, PAD), pl.ds(pl.multiple_of(start + PAD + 480, 16), PAD)]
    xh = jnp.concatenate([xc[i, r, :] for i in range(4) for r in ends], axis=0)
    for p in range(5):
        y = jnp.dot(xh, weights(p), preferred_element_type=f32)
        for i in range(4):
            for h, r in enumerate((0, PAD + 480)):
                o = (2 * i + h) * PAD
                y_taps[i, 2 * p, r : r + PAD, :] = y[o : o + PAD, :128]
                if p < 4:
                    y_taps[i, 2 * p + 1, r : r + PAD, :] = y[o : o + PAD, 128:]

    for i in range(4):
        finish(i, (0, 3))

    for c in small[2:]:
        c.wait()
    cwt = cw[...]
    pool = pooled[...]
    part = jnp.zeros((8, 128), f32)
    for s in range(5):
        t = jnp.sum(pool * cwt[s : s + 1, :], axis=1, keepdims=True)
        part = jnp.where(lane[0:8] == s, t[0:8], part)
        part = jnp.where(lane[0:8] == 16 + s, t[8:16], part)
    logit[cc, xx] = part
    logit_copies = []
    for d in (2, 1, 3, 0):
        for c in range(2):
            if d:
                dev = (yy, zz * 2 + c, lax.rem(xx + d, nx))
            elif c == 0:
                dev = partner
            else:
                continue
            k = len(logit_copies)
            logit_copies.append(
                remote(logit.at[cc, xx], logit.at[cc, xx], logit_send.at[k], logit_recv.at[cc, xx], dev)
            )
    for c in logit_copies:
        c.start()

    to_partner(deriv, pl.ds(start, EPOCH))
    to_partner(deriv, pl.ds(pl.multiple_of(start + 3 * EPOCH, 8), EPOCH))

    pl.semaphore_wait(known1, 4)
    for dev in (along_z(6), along_z(2)):
        tell(known2, dev)

    pair_copies[1].wait_recv()
    for i in range(4):
        xt[i] = xc[i].T
    for d in nearby:
        s = lax.rem(yy + d, ny)
        arrived(teach.at[s], teach_recv.at[s])
    nights = [night[i].astype(f32) for i in range(4)]
    lane8 = lane[0:8]
    sums = [jnp.zeros((8, 128), f32) for _ in range(4)]
    for d in (0, *nearby):
        t = teach[lax.rem(yy + d, ny)]
        of = jnp.where(lane8 < 16, t[:, 8:9], t[:, 24:25])
        for i in range(4):
            sums[i] = sums[i] + jnp.where(of == nights[i], t, 0.0)
    soft = []
    for i in range(4):
        s = sums[i] + pltpu.roll(sums[i], 112, 1)
        s = s[0:4] + s[4:8]
        soft.append(s / s[:, 9:10])
    soft = jnp.concatenate(soft, axis=0)
    label = jnp.zeros((16, 128), i32)
    for i in range(4):
        for e in range(4):
            label = jnp.where(row == 4 * i + e, labels[e, night[i]], label)
    goal[cc] = 0.5 * soft + 0.5 * (lane == label).astype(f32)
    goal_copy = remote(goal.at[cc], goal.at[cc], pair_send.at[5], pair_recv.at[5], partner)
    goal_copy.start()

    for d in range(1, 4):
        s = lax.rem(xx + d, nx)
        for c in range(2):
            arrived(logit.at[c, s], logit_recv.at[c, s])
    arrived(logit.at[oc, xx], logit_recv.at[oc, xx])
    goal_copy.wait_recv()
    shift = jnp.zeros((16, 128), f32)
    for s in range(5):
        shift = shift + jnp.where(lane == s, bias[s], 0.0)
    slopes, both = [], []
    for b in range(2):
        logits = logit[b, 0] + logit[b, 1] + logit[b, 2] + logit[b, 3]
        logits = jnp.concatenate([logits, pltpu.roll(logits, 112, 1)], axis=0) + shift
        both.append(logits)
        expo = jnp.where(lane < 5, jnp.exp(logits), 0.0)
        diff = expo / jnp.sum(expo, axis=1, keepdims=True) - goal[b]
        slope = jnp.zeros((16, 128), f32)
        for s in range(5):
            slope = slope + diff[:, s : s + 1] * cwt[s : s + 1, :]
        slopes.append(slope)
    logits = jnp.where(cc == 0, both[0], both[1])
    for i in range(4):
        logits_out[i] = logits[4 * i : 4 * i + 4, :5]

    for c in pair_copies[2:]:
        c.wait_recv()
    for i in range(4):
        for b in range(2):
            for e in range(4):
                o = 480 * b + EPOCH * e
                up[i, pl.ds(24 + o, EPOCH), :] = (
                    deriv[i, pl.ds(o, EPOCH), :] * slopes[b][4 * i + e : 4 * i + e + 1, :]
                )

    def backward(taps, channels, at):
        acc = None
        for i in range(4):
            us = [up[i, pl.ds(12 - k, LONG), :].astype(bf16) for k in taps]
            u = us[0] if len(us) == 1 else jnp.concatenate(us, axis=1)
            g = jnp.dot(xt[i, channels, :], u, preferred_element_type=f32)
            acc = g if acc is None else acc + g
        for n in range(len(taps)):
            grad[pl.ds(at + acc.shape[0] * n, acc.shape[0]), :] = acc[:, 128 * n : 128 * n + 128]

    @pl.when(cc == 0)
    def _():
        backward((0, 1), slice(None), 0)
        backward((2, 3), slice(None), 512)
        backward((4,), slice(0, 128), 1024)

    @pl.when(cc == 1)
    def _():
        backward((4,), slice(128, 256), 0)
        backward((5, 6), slice(None), 128)
        backward((7, 8), slice(None), 640)

    power = jnp.ceil(jnp.log2(jnp.maximum(jnp.max(jnp.abs(grad[...]), axis=0, keepdims=True), 1e-30)) + 0.01)
    factor = jnp.exp2(15.0 - power)
    power = jnp.broadcast_to(power, (8, 128))

    def code(slot, units):
        t = jnp.concatenate([grad[pl.ds(288 * y + UNIT * z, UNIT), :] for y, z in units], axis=0)
        tx[slot] = jnp.concatenate([jnp.round(t * factor), power], axis=0).astype(i32).astype(i16)

    pl.semaphore_wait(known2, 2)
    half_y, half_z = yy // 4 == cc, zz // 4
    copies = []

    def send(copy, sent):
        copies.append((copy, sent))
        pl.when(sent)(copy.start)

    far_first = ((2, 0), (3, 1), (1, 3), (0, 2))
    for h in range(2):
        for j in range(4):
            code(2 * j + h, [(j, j % 2 + 4 * h), (j, j % 2 + 4 * h + 2)])
        for m, (near, far) in enumerate(far_first):
            j = lax.rem(yy + jnp.where(half_y, near, far), 4)
            dev = (4 * cc + j, zz * 2 + h, xx)
            send(
                remote(tx.at[2 * j + h], rx.at[yy], send1.at[4 * h + m], recv1.at[yy], dev),
                jnp.logical_not((yy == 4 * cc + j) & (cc == h)),
            )
        for z in range(4 * h, 4 * h + 4):
            code(8 + z, [(1 - z % 2, z), (3 - z % 2, z)])
        for m, (near, far) in enumerate(far_first):
            z = 4 * h + lax.rem(zz + jnp.where(half_z == h, near, far), 4)
            dev = (yy, z * 2 + cc, xx)
            send(
                remote(tx.at[8 + z], rx.at[8 + zz], send1.at[8 + 4 * h + m], recv1.at[8 + zz], dev),
                zz != z,
            )

    @pl.when(half_y)
    def _():
        rx[yy] = tx[2 * lax.rem(yy, 4) + cc]

    rx[8 + zz] = tx[8 + zz]

    handed = []
    for k in range(2):
        for m in range(4):
            if k == 0:
                own, dev = zz, (yy, (yy % 2 + 4 * cc + 2 * (m // 2)) * 2 + m % 2, xx)
            else:
                own, dev = yy, (4 * cc + 1 - zz % 2 + 2 * (m // 2), zz * 2 + m % 2, xx)
            slot = 4 * k + m
            copy = remote(tx2.at[slot], rx2.at[own], send2.at[slot], recv2.at[own], dev)
            handed.append((copy, (dev[0] != yy) | (dev[1] != tm), own))

    def hand_out(k):
        acc = jnp.zeros((WIDE, 128), f32)
        for s in range(8):
            if k == 0:
                @pl.when(jnp.logical_not(half_y & (yy == s)))
                def _():
                    arrived(rx.at[s], recv1.at[s])
            else:
                @pl.when(zz != s)
                def _():
                    arrived(rx.at[8 + s], recv1.at[8 + s])
        for s in range(8 * k, 8 * k + 8):
            t = rx[s].astype(f32)
            acc = acc + t[:WIDE] * jnp.exp2(t[WIDE : WIDE + 1] - 15.0)
        piece[0:WIDE, :] = acc
        piece[WIDE:, :] = jnp.zeros((8, 128), f32)
        for slot in range(4 * k, 4 * k + 4):
            copy, sent, own = handed[slot]
            tx2[slot] = piece[pl.ds(18 * (slot % 4), 24), :]
            pl.when(sent)(copy.start)

            @pl.when(jnp.logical_not(sent))
            def _():
                rx2[own] = tx2[slot]

    @pl.when(cc == 0)
    def _():
        hand_out(0)
        hand_out(1)

    @pl.when(cc == 1)
    def _():
        hand_out(1)
        hand_out(0)

    copies += [(copy, sent) for copy, sent, _ in handed]
    even = (yy + zz) % 2 == 0
    holder = jnp.where(even, half_z, yy // 4)
    place = jnp.where(even, zz, yy)
    for s in range(8):
        @pl.when(jnp.logical_not((place == s) & (holder == cc)))
        def _():
            arrived(rx2.at[s], recv2.at[s])
    out = rx2[0]
    for s in range(1, 8):
        out = out + rx2[s]
    grad_out[...] = out[:18] * (1.0 / 32)

    @pl.when(has_next)
    def _():
        for c in halo_copies:
            c.wait_send()

    for c in pair_copies + [goal_copy] + teach_copies + logit_copies:
        c.wait_send()
    for c, sent in copies:
        pl.when(sent)(c.wait_send)


def local(activations, conv_weight, class_weight, class_bias, teacher_logits, night_of, section_labels):
    hbm = pl.BlockSpec(memory_space=pltpu.HBM)
    vm = pl.BlockSpec(memory_space=pltpu.VMEM)
    dma = pltpu.SemaphoreType.DMA
    return pl.pallas_call(
        kernel,
        out_shape=(pltpu.VMEM((4, 4, 5), f32), pltpu.VMEM((18, 128), f32)),
        in_specs=[hbm] * 7,
        out_specs=(vm, vm),
        scratch_shapes=[
            pltpu.VMEM((5, 128), f32),
            pltpu.VMEM((4, 4, 5), f32),
            pltpu.SMEM((4,), i32),
            pltpu.SMEM((4, 8), i32),
            pltpu.SMEM((5,), f32),
            pltpu.VMEM((4, LONG, 256), bf16),
            pltpu.VMEM((2304, 128), bf16),
            pltpu.VMEM((4, 9, 512, 128), f32),
            pltpu.VMEM((4, 960, 128), f32),
            pltpu.VMEM((16, 128), f32),
            pltpu.VMEM((4, LONG + 16, 128), f32),
            pltpu.VMEM((4, 256, LONG), bf16),
            pltpu.VMEM((1152, 128), f32),
            pltpu.VMEM((8, 8, 128), f32),
            pltpu.VMEM((2, 16, 128), f32),
            pltpu.VMEM((2, 4, 8, 128), f32),
            pltpu.VMEM((16, WIDE + 8, 128), i16),
            pltpu.VMEM((16, WIDE + 8, 128), i16),
            pltpu.VMEM((WIDE + 8, 128), f32),
            pltpu.VMEM((8, 24, 128), f32),
            pltpu.VMEM((8, 24, 128), f32),
            dma((5,)), dma((5,)),
            dma((2,)), dma((2,)),
            dma((6,)), dma((6,)),
            dma((4,)), dma((8,)),
            dma((7,)), dma((2, 4)),
            dma((16,)), dma((16,)),
            dma((8,)), dma((8,)),
            pltpu.SemaphoreType.REGULAR, pltpu.SemaphoreType.REGULAR,
        ],
        compiler_params=pltpu.CompilerParams(
            collective_id=0, has_side_effects=True, vmem_limit_bytes=63 << 20
        ),
    )(activations, conv_weight, class_weight.T, teacher_logits, night_of, section_labels.T, class_bias)


def solution(mesh):
    in_specs = (
        P("inst", "tm", None),
        P(None, "filt"),
        P("filt", None),
        P(),
        P("inst", "tm", None),
        P("inst"),
        P(None, "tm"),
    )
    out_specs = (P("inst", "tm", None), P(("inst", "tm"), "filt"))
    return jax.shard_map(local, mesh=mesh, in_specs=in_specs, out_specs=out_specs, check_vma=False)
```

```python
import functools

import jax
import jax.numpy as jnp
from jax import lax
from jax.experimental import pallas as pl
from jax.experimental.pallas import tpu as pltpu
from jax.sharding import PartitionSpec as P

f32, bf16, i32, i16 = jnp.float32, jnp.bfloat16, jnp.int32, jnp.int16
MESH = pl.DeviceIdType.MESH
EPOCH = 120
PAD = 16
UNIT = 36
WIDE = 2 * UNIT
LONG = 1024
TN = False


def kernel(
    x, w, cw_hbm, tl_hbm, night_hbm, labels_hbm, bias_hbm,
    logits_out, grad_out,
    cw, tl, night, labels, bias,
    xc, wv, y_taps, deriv, pooled, up, xt, grad,
    teach, goal, logit, tx, rx, piece, tx2, rx2,
    small_sem, load_sem, halo_send, halo_recv, pair_send, pair_recv,
    teach_send, teach_recv, logit_send, logit_recv, send1, recv1, send2, recv2, known1, known2,
):
    yy, tm, xx = lax.axis_index("inst"), lax.axis_index("tm"), lax.axis_index("filt")
    zz, cc = tm // 2, tm % 2
    oc = 1 - cc
    ny, nz, nx = 8, 8, 4

    def remote(src, dst, ssem, rsem, dev):
        return pltpu.make_async_remote_copy(
            src_ref=src, dst_ref=dst, send_sem=ssem, recv_sem=rsem, device_id=dev, device_id_type=MESH
        )

    def arrived(dst, rsem):
        remote(dst, dst, rsem, rsem, (yy, tm, xx)).wait_recv()

    barrier = pltpu.get_barrier_semaphore()

    def greet(dev):
        pl.semaphore_signal(barrier, inc=1, device_id=dev, device_id_type=MESH)

    def greet_z(d):
        for c in range(2):
            greet((yy, lax.rem(zz + d, nz) * 2 + c, xx))

    def greet_y(d):
        for c in range(2):
            greet((lax.rem(yy + d, ny), zz * 2 + c, xx))

    greet_z(7)
    greet_z(1)
    greet((yy, zz * 2 + oc, xx))
    for d in range(1, 4):
        for c in range(2):
            greet((yy, zz * 2 + c, lax.rem(xx + d, nx)))
    for d in (1, 7, 2, 6):
        greet_y(d)

    start = pl.multiple_of(480 * cc, 16)
    own = pl.ds(pl.multiple_of(PAD + 480 * cc, 16), 480)
    pairs = [(tl_hbm, tl), (night_hbm, night), (cw_hbm, cw), (labels_hbm, labels), (bias_hbm, bias)]
    small = [pltpu.make_async_copy(src, dst, small_sem.at[i]) for i, (src, dst) in enumerate(pairs)]
    loads = [pltpu.make_async_copy(w, wv, load_sem.at[4])]
    loads += [
        pltpu.make_async_copy(x.at[i], xc.at[i, own], load_sem.at[i]) for i in range(4)
    ]
    for c in small + loads:
        c.start()

    small[0].wait()
    small[1].wait()
    row = lax.broadcasted_iota(i32, (16, 128), 0)
    lane = lax.broadcasted_iota(i32, (16, 128), 1)
    t5 = jnp.concatenate([tl[i] for i in range(4)], axis=0)
    t5 = jnp.exp(t5 - jnp.max(t5, axis=1, keepdims=True))
    t5 = t5 / jnp.sum(t5, axis=1, keepdims=True)
    tile = jnp.zeros((16, 128), f32)
    for s in range(5):
        tile = jnp.where(lane == s, t5[:, s : s + 1], tile)
    for i in range(4):
        tile = jnp.where((lane == 8) & (row // 4 == i), night[i].astype(f32), tile)
    tile = jnp.where(lane == 9, 1.0, tile)
    teach[yy] = tile[0:8] + pltpu.roll(tile[8:16], 16, 1)

    @pl.when(zz == 0)
    def _():
        for i in range(4):
            xc[i, 0:PAD, :] = jnp.zeros((PAD, 256), bf16)

    @pl.when(zz == nz - 1)
    def _():
        for i in range(4):
            xc[i, PAD + 960 : 2 * PAD + 960, :] = jnp.zeros((PAD, 256), bf16)

    for i in range(4):
        xc[i, 2 * PAD + 960 :, :] = jnp.zeros((LONG - 2 * PAD - 960, 256), bf16)
        up[i, 0:24, :] = jnp.zeros((24, 128), f32)
        up[i, 984:, :] = jnp.zeros((56, 128), f32)

    def weights(p):
        if p == 4:
            return wv[pl.ds(2048, 256), :]
        return jnp.concatenate([wv[pl.ds(512 * p, 256), :], wv[pl.ds(512 * p + 256, 256), :]], axis=1)

    def forward(i):
        for p in range(5):
            y = jnp.dot(xc[i, own, :], weights(p), preferred_element_type=f32)
            y_taps[i, 2 * p, PAD : PAD + 480, :] = y[:, :128]
            if p < 4:
                y_taps[i, 2 * p + 1, PAD : PAD + 480, :] = y[:, 128:]

    def finish(i, at, count):
        o = PAD - 4 + at
        pre = y_taps[i, 0, pl.ds(o, count), :]
        for k in range(1, 9):
            pre = pre + y_taps[i, k, pl.ds(o + k, count), :]
        ex = jnp.exp(jnp.minimum(pre, 0.0))
        act = jnp.where(pre > 0, pre, ex - 1.0)
        deriv[i, pl.ds(pl.multiple_of(start + at, 8), count), :] = ex
        return jnp.sum(act, axis=0, keepdims=True) * (1.0 / EPOCH)

    for c in loads:
        c.wait()
    pl.semaphore_wait(barrier, 19)

    def tell(sem, dev):
        pl.semaphore_signal(sem, inc=1, device_id=dev, device_id_type=MESH)

    def along_y(d):
        return (lax.rem(yy + d, ny), tm, xx)

    def along_z(d):
        return (yy, lax.rem(zz + d, nz) * 2 + cc, xx)

    partner = (yy, zz * 2 + oc, xx)
    pair_copies = []

    def to_partner(ref, rows):
        k = len(pair_copies)
        c = remote(ref.at[:, rows], ref.at[:, rows], pair_send.at[k], pair_recv.at[k], partner)
        c.start()
        pair_copies.append(c)

    halo_src = pl.ds(pl.multiple_of(PAD + 944 * cc, 16), PAD)
    halo_dst = pl.ds(pl.multiple_of((PAD + 960) * oc, 16), PAD)
    has_next = jnp.where(cc == 0, zz > 0, zz < nz - 1)
    halo_copies = [
        remote(
            xc.at[:, halo_src], xc.at[:, halo_dst], halo_send.at[c], halo_recv.at[oc],
            (yy, (zz - 1 + 2 * cc) * 2 + c, xx),
        )
        for c in range(2)
    ]

    @pl.when(has_next)
    def _():
        for c in halo_copies:
            c.start()

    nearby = (2, 6, 1, 7)
    teach_copies = [
        remote(teach.at[yy], teach.at[yy], teach_send.at[k], teach_recv.at[yy], (lax.rem(yy + d, ny), tm, xx))
        for k, d in enumerate(nearby)
    ]
    for c in teach_copies:
        c.start()
    to_partner(xc, pl.ds(pl.multiple_of(480 + 16 * cc, 16), PAD))
    for dev in (along_z(7), along_z(1), along_y(2), along_y(6)):
        tell(known1, dev)

    for i in range(4):
        forward(i)
        for e, at, count in ((0, 8, EPOCH - 8), (1, EPOCH, EPOCH), (2, 2 * EPOCH, EPOCH), (3, 3 * EPOCH, EPOCH - 8)):
            pooled[pl.ds(4 * i + e, 1), :] = finish(i, at, count)

    to_partner(xc, pl.ds(pl.multiple_of(PAD + 496 * cc, 16), 464))
    to_partner(deriv, pl.ds(pl.multiple_of(start + 8, 8), 464))
    pair_copies[0].wait_recv()

    @pl.when(zz > 0)
    def _():
        arrived(xc.at[:, pl.ds(0, PAD)], halo_recv.at[0])

    @pl.when(zz < nz - 1)
    def _():
        arrived(xc.at[:, pl.ds(PAD + 960, PAD)], halo_recv.at[1])

    ends = [pl.ds(start, PAD), pl.ds(pl.multiple_of(start + PAD + 480, 16), PAD)]
    xh = jnp.concatenate([xc[i, r, :] for i in range(4) for r in ends], axis=0)
    for p in range(5):
        y = jnp.dot(xh, weights(p), preferred_element_type=f32)
        for i in range(4):
            for h, r in enumerate((0, PAD + 480)):
                o = (2 * i + h) * PAD
                y_taps[i, 2 * p, r : r + PAD, :] = y[o : o + PAD, :128]
                if p < 4:
                    y_taps[i, 2 * p + 1, r : r + PAD, :] = y[o : o + PAD, 128:]

    for i in range(4):
        for e, at in ((0, 0), (3, 472)):
            pooled[pl.ds(4 * i + e, 1), :] += finish(i, at, 8)

    for c in small[2:]:
        c.wait()
    cwt = cw[...]
    pool = pooled[...]
    part = jnp.zeros((8, 128), f32)
    for s in range(5):
        t = jnp.sum(pool * cwt[s : s + 1, :], axis=1, keepdims=True)
        part = jnp.where(lane[0:8] == s, t[0:8], part)
        part = jnp.where(lane[0:8] == 16 + s, t[8:16], part)
    logit[cc, xx] = part
    logit_copies = []
    for d in (2, 1, 3, 0):
        for c in range(2):
            if d:
                dev = (yy, zz * 2 + c, lax.rem(xx + d, nx))
            elif c == 0:
                dev = partner
            else:
                continue
            k = len(logit_copies)
            logit_copies.append(
                remote(logit.at[cc, xx], logit.at[cc, xx], logit_send.at[k], logit_recv.at[cc, xx], dev)
            )
    for c in logit_copies:
        c.start()

    to_partner(deriv, pl.ds(start, 8))
    to_partner(deriv, pl.ds(pl.multiple_of(start + 472, 8), 8))


    pair_copies[1].wait_recv()
    for i in range(4):
        xt[i] = xc[i].T
    pl.semaphore_wait(known1, 4)
    for dev in (along_z(6), along_z(2)):
        tell(known2, dev)
    for d in nearby:
        s = lax.rem(yy + d, ny)
        arrived(teach.at[s], teach_recv.at[s])
    nights = [night[i].astype(f32) for i in range(4)]
    lane8 = lane[0:8]
    sums = [jnp.zeros((8, 128), f32) for _ in range(4)]
    for d in (0, *nearby):
        t = teach[lax.rem(yy + d, ny)]
        of = jnp.where(lane8 < 16, t[:, 8:9], t[:, 24:25])
        for i in range(4):
            sums[i] = sums[i] + jnp.where(of == nights[i], t, 0.0)
    soft = []
    for i in range(4):
        s = sums[i] + pltpu.roll(sums[i], 112, 1)
        s = s[0:4] + s[4:8]
        soft.append(s / s[:, 9:10])
    soft = jnp.concatenate(soft, axis=0)
    label = jnp.zeros((16, 128), i32)
    for i in range(4):
        for e in range(4):
            label = jnp.where(row == 4 * i + e, labels[e, night[i]], label)
    goal[cc] = 0.5 * soft + 0.5 * (lane == label).astype(f32)
    goal_copy = remote(goal.at[cc], goal.at[cc], pair_send.at[5], pair_recv.at[5], partner)
    goal_copy.start()

    for d in range(1, 4):
        s = lax.rem(xx + d, nx)
        for c in range(2):
            arrived(logit.at[c, s], logit_recv.at[c, s])
    arrived(logit.at[oc, xx], logit_recv.at[oc, xx])
    goal_copy.wait_recv()
    shift = jnp.zeros((16, 128), f32)
    for s in range(5):
        shift = shift + jnp.where(lane == s, bias[s], 0.0)
    slopes, both = [], []
    for b in range(2):
        logits = logit[b, 0] + logit[b, 1] + logit[b, 2] + logit[b, 3]
        logits = jnp.concatenate([logits, pltpu.roll(logits, 112, 1)], axis=0) + shift
        both.append(logits)
        expo = jnp.where(lane < 5, jnp.exp(logits), 0.0)
        diff = expo / jnp.sum(expo, axis=1, keepdims=True) - goal[b]
        slope = jnp.zeros((16, 128), f32)
        for s in range(5):
            slope = slope + diff[:, s : s + 1] * cwt[s : s + 1, :]
        slopes.append(slope)
    logits = jnp.where(cc == 0, both[0], both[1])
    for i in range(4):
        logits_out[i] = logits[4 * i : 4 * i + 4, :5]

    for c in pair_copies[2:]:
        c.wait_recv()
    for i in range(4):
        for b in range(2):
            for e in range(4):
                o = 480 * b + EPOCH * e
                up[i, pl.ds(24 + o, EPOCH), :] = (
                    deriv[i, pl.ds(o, EPOCH), :] * slopes[b][4 * i + e : 4 * i + e + 1, :]
                )

    def backward(taps, channels, at):
        acc = None
        for i in range(4):
            us = [up[i, pl.ds(12 - k, LONG), :].astype(bf16) for k in taps]
            u = us[0] if len(us) == 1 else jnp.concatenate(us, axis=1)
            g = jnp.dot(xt[i, channels, :], u, preferred_element_type=f32)
            acc = g if acc is None else acc + g
        for n in range(len(taps)):
            grad[pl.ds(at + acc.shape[0] * n, acc.shape[0]), :] = acc[:, 128 * n : 128 * n + 128]

    @pl.when(cc == 0)
    def _():
        backward((0, 1), slice(None), 0)
        backward((2, 3), slice(None), 512)
        backward((4,), slice(0, 128), 1024)

    @pl.when(cc == 1)
    def _():
        backward((4,), slice(128, 256), 0)
        backward((5, 6), slice(None), 128)
        backward((7, 8), slice(None), 640)

    power = jnp.ceil(jnp.log2(jnp.maximum(jnp.max(jnp.abs(grad[...]), axis=0, keepdims=True), 1e-30)) + 0.01)
    factor = jnp.exp2(15.0 - power)
    power = jnp.broadcast_to(power, (8, 128))

    def code(slot, units):
        t = jnp.concatenate([grad[pl.ds(288 * y + UNIT * z, UNIT), :] for y, z in units], axis=0)
        tx[slot] = jnp.concatenate([jnp.round(t * factor), power], axis=0).astype(i32).astype(i16)

    pl.semaphore_wait(known2, 2)
    half_y, half_z = yy // 4 == cc, zz // 4
    copies = []

    def send(copy, sent):
        copies.append((copy, sent))
        copy.start() if sent is True else pl.when(sent)(copy.start)

    far_first = ((2, 0), (3, 1), (1, 3), (0, 2))
    for h in range(2):
        for j in range(4):
            code(2 * j + h, [(j, j % 2 + 4 * h), (j, j % 2 + 4 * h + 2)])
        for m, (near, far) in enumerate(far_first):
            j = lax.rem(yy + jnp.where(half_y, near, far), 4)
            dev = (4 * cc + j, zz * 2 + (oc if h else cc), xx)
            send(
                remote(tx.at[2 * j + h], rx.at[yy], send1.at[4 * h + m], recv1.at[yy], dev),
                True if h else yy != 4 * cc + j,
            )
        for z in range(4 * h, 4 * h + 4):
            code(8 + z, [(1 - z % 2, z), (3 - z % 2, z)])
        for m, (near, far) in enumerate(far_first):
            z = 4 * h + lax.rem(zz + jnp.where(half_z == h, near, far), 4)
            dev = (yy, z * 2 + cc, xx)
            send(
                remote(tx.at[8 + z], rx.at[8 + zz], send1.at[8 + 4 * h + m], recv1.at[8 + zz], dev),
                zz != z,
            )

    @pl.when(half_y)
    def _():
        rx[yy] = tx[2 * lax.rem(yy, 4)]

    rx[8 + zz] = tx[8 + zz]

    handed = []
    for k in range(2):
        for m in range(4):
            if k == 0:
                own, dev = zz, (yy, (yy % 2 + jnp.where(half_y, 0, 4) + 2 * (m // 2)) * 2 + m % 2, xx)
            else:
                own, dev = yy, (4 * cc + 1 - zz % 2 + 2 * (m // 2), zz * 2 + m % 2, xx)
            slot = 4 * k + m
            copy = remote(tx2.at[slot], rx2.at[own], send2.at[slot], recv2.at[own], dev)
            handed.append((copy, (dev[0] != yy) | (dev[1] != tm), own))

    def hand_out(k):
        acc = jnp.zeros((WIDE, 128), f32)
        for s in range(8):
            if k == 0:
                @pl.when(jnp.logical_not(half_y & (yy == s)))
                def _():
                    arrived(rx.at[s], recv1.at[s])
            else:
                @pl.when(zz != s)
                def _():
                    arrived(rx.at[8 + s], recv1.at[8 + s])
        for s in range(8 * k, 8 * k + 8):
            t = rx[s].astype(f32)
            acc = acc + t[:WIDE] * jnp.exp2(t[WIDE : WIDE + 1] - 15.0)
        piece[0:WIDE, :] = acc
        piece[WIDE:, :] = jnp.zeros((8, 128), f32)
        for slot in range(4 * k, 4 * k + 4):
            copy, sent, own = handed[slot]
            tx2[slot] = piece[pl.ds(18 * (slot % 4), 24), :]
            pl.when(sent)(copy.start)

            @pl.when(jnp.logical_not(sent))
            def _():
                rx2[own] = tx2[slot]

    z_first = jnp.logical_not(half_y) | (zz < 4)

    @pl.when(jnp.logical_not(z_first))
    def _():
        hand_out(0)
        hand_out(1)

    @pl.when(z_first)
    def _():
        hand_out(1)
        hand_out(0)

    copies += [(copy, sent) for copy, sent, _ in handed]
    even = (yy + zz) % 2 == 0
    holder = jnp.where(even & (half_z == 1), 1 - yy // 4, yy // 4)
    place = jnp.where(even, zz, yy)
    for s in range(8):
        @pl.when(jnp.logical_not((place == s) & (holder == cc)))
        def _():
            arrived(rx2.at[s], recv2.at[s])
    out = rx2[0]
    for s in range(1, 8):
        out = out + rx2[s]
    grad_out[...] = out[:18] * (1.0 / 32)

    @pl.when(has_next)
    def _():
        for c in halo_copies:
            c.wait_send()

    for c in pair_copies + [goal_copy] + teach_copies + logit_copies:
        c.wait_send()
    for c, sent in copies:
        c.wait_send() if sent is True else pl.when(sent)(c.wait_send)


def local(activations, conv_weight, class_weight, class_bias, teacher_logits, night_of, section_labels):
    hbm = pl.BlockSpec(memory_space=pltpu.HBM)
    vm = pl.BlockSpec(memory_space=pltpu.VMEM)
    dma = pltpu.SemaphoreType.DMA
    return pl.pallas_call(
        kernel,
        out_shape=(pltpu.VMEM((4, 4, 5), f32), pltpu.VMEM((18, 128), f32)),
        in_specs=[hbm] * 7,
        out_specs=(vm, vm),
        scratch_shapes=[
            pltpu.VMEM((5, 128), f32),
            pltpu.VMEM((4, 4, 5), f32),
            pltpu.SMEM((4,), i32),
            pltpu.SMEM((4, 8), i32),
            pltpu.SMEM((5,), f32),
            pltpu.VMEM((4, LONG, 256), bf16),
            pltpu.VMEM((2304, 128), bf16),
            pltpu.VMEM((4, 9, 512, 128), f32),
            pltpu.VMEM((4, 960, 128), f32),
            pltpu.VMEM((16, 128), f32),
            pltpu.VMEM((4, LONG + 16, 128), f32),
            pltpu.VMEM((4, 256, LONG), bf16),
            pltpu.VMEM((1152, 128), f32),
            pltpu.VMEM((8, 8, 128), f32),
            pltpu.VMEM((2, 16, 128), f32),
            pltpu.VMEM((2, 4, 8, 128), f32),
            pltpu.VMEM((16, WIDE + 8, 128), i16),
            pltpu.VMEM((16, WIDE + 8, 128), i16),
            pltpu.VMEM((WIDE + 8, 128), f32),
            pltpu.VMEM((8, 24, 128), f32),
            pltpu.VMEM((8, 24, 128), f32),
            dma((5,)), dma((5,)),
            dma((2,)), dma((2,)),
            dma((6,)), dma((6,)),
            dma((4,)), dma((8,)),
            dma((7,)), dma((2, 4)),
            dma((16,)), dma((16,)),
            dma((8,)), dma((8,)),
            pltpu.SemaphoreType.REGULAR, pltpu.SemaphoreType.REGULAR,
        ],
        compiler_params=pltpu.CompilerParams(
            collective_id=0, has_side_effects=True, vmem_limit_bytes=63 << 20
        ),
    )(activations, conv_weight, class_weight.T, teacher_logits, night_of, section_labels.T, class_bias)


def solution(mesh):
    in_specs = (
        P("inst", "tm", None),
        P(None, "filt"),
        P("filt", None),
        P(),
        P("inst", "tm", None),
        P("inst"),
        P(None, "tm"),
    )
    out_specs = (P("inst", "tm", None), P(("inst", "tm"), "filt"))
    return jax.shard_map(local, mesh=mesh, in_specs=in_specs, out_specs=out_specs, check_vma=False)
```

```python
import functools

import jax
import jax.numpy as jnp
from jax import lax
from jax.experimental import pallas as pl
from jax.experimental.pallas import tpu as pltpu
from jax.sharding import PartitionSpec as P

f32, bf16, i32, i16 = jnp.float32, jnp.bfloat16, jnp.int32, jnp.int16
MESH = pl.DeviceIdType.MESH
EPOCH = 120
PAD = 16
UNIT = 36
WIDE = 2 * UNIT
LONG = 1024
TN = False


def kernel(
    x, w, cw_hbm, tl_hbm, night_hbm, labels_hbm, bias_hbm,
    logits_out, grad_out,
    cw, tl, night, labels, bias,
    xc, wv, y_taps, deriv, pooled, up, xt, grad,
    teach, goal, logit, tx, rx, piece, tx2, rx2,
    small_sem, load_sem, halo_send, halo_recv, pair_send, pair_recv,
    teach_send, teach_recv, logit_send, logit_recv, send1, recv1, send2, recv2, known1, known2,
):
    yy, tm, xx = lax.axis_index("inst"), lax.axis_index("tm"), lax.axis_index("filt")
    zz, cc = tm // 2, tm % 2
    oc = 1 - cc
    ny, nz, nx = 8, 8, 4

    def remote(src, dst, ssem, rsem, dev):
        return pltpu.make_async_remote_copy(
            src_ref=src, dst_ref=dst, send_sem=ssem, recv_sem=rsem, device_id=dev, device_id_type=MESH
        )

    def arrived(dst, rsem):
        remote(dst, dst, rsem, rsem, (yy, tm, xx)).wait_recv()

    barrier = pltpu.get_barrier_semaphore()

    def greet(dev):
        pl.semaphore_signal(barrier, inc=1, device_id=dev, device_id_type=MESH)

    def greet_z(d):
        for c in range(2):
            greet((yy, lax.rem(zz + d, nz) * 2 + c, xx))

    def greet_y(d):
        for c in range(2):
            greet((lax.rem(yy + d, ny), zz * 2 + c, xx))

    greet_z(7)
    greet_z(1)
    greet((yy, zz * 2 + oc, xx))
    for d in range(1, 4):
        for c in range(2):
            greet((yy, zz * 2 + c, lax.rem(xx + d, nx)))
    for d in (1, 7, 2, 6):
        greet_y(d)

    start = pl.multiple_of(480 * cc, 16)
    own = pl.ds(pl.multiple_of(PAD + 480 * cc, 16), 480)
    pairs = [(tl_hbm, tl), (night_hbm, night), (cw_hbm, cw), (labels_hbm, labels), (bias_hbm, bias)]
    small = [pltpu.make_async_copy(src, dst, small_sem.at[i]) for i, (src, dst) in enumerate(pairs)]
    loads = [pltpu.make_async_copy(w, wv, load_sem.at[4])]
    loads += [
        pltpu.make_async_copy(x.at[i], xc.at[i, own], load_sem.at[i]) for i in range(4)
    ]
    for c in small + loads:
        c.start()

    small[0].wait()
    small[1].wait()
    row = lax.broadcasted_iota(i32, (16, 128), 0)
    lane = lax.broadcasted_iota(i32, (16, 128), 1)
    t5 = jnp.concatenate([tl[i] for i in range(4)], axis=0)
    t5 = jnp.exp(t5 - jnp.max(t5, axis=1, keepdims=True))
    t5 = t5 / jnp.sum(t5, axis=1, keepdims=True)
    tile = jnp.zeros((16, 128), f32)
    for s in range(5):
        tile = jnp.where(lane == s, t5[:, s : s + 1], tile)
    for i in range(4):
        tile = jnp.where((lane == 8) & (row // 4 == i), night[i].astype(f32), tile)
    tile = jnp.where(lane == 9, 1.0, tile)
    teach[yy] = tile[0:8] + pltpu.roll(tile[8:16], 16, 1)

    @pl.when(zz == 0)
    def _():
        for i in range(4):
            xc[i, 0:PAD, :] = jnp.zeros((PAD, 256), bf16)

    @pl.when(zz == nz - 1)
    def _():
        for i in range(4):
            xc[i, PAD + 960 : 2 * PAD + 960, :] = jnp.zeros((PAD, 256), bf16)

    for i in range(4):
        xc[i, 2 * PAD + 960 :, :] = jnp.zeros((LONG - 2 * PAD - 960, 256), bf16)
        up[i, 0:24, :] = jnp.zeros((24, 128), f32)
        up[i, 984:, :] = jnp.zeros((56, 128), f32)

    def weights(p):
        if p == 4:
            return wv[pl.ds(2048, 256), :]
        return jnp.concatenate([wv[pl.ds(512 * p, 256), :], wv[pl.ds(512 * p + 256, 256), :]], axis=1)

    def forward(i):
        for p in range(5):
            y = jnp.dot(xc[i, own, :], weights(p), preferred_element_type=f32)
            y_taps[i, 2 * p, PAD : PAD + 480, :] = y[:, :128]
            if p < 4:
                y_taps[i, 2 * p + 1, PAD : PAD + 480, :] = y[:, 128:]

    def finish(i, at, count):
        o = PAD - 4 + at
        pre = y_taps[i, 0, pl.ds(o, count), :]
        for k in range(1, 9):
            pre = pre + y_taps[i, k, pl.ds(o + k, count), :]
        ex = jnp.exp(jnp.minimum(pre, 0.0))
        act = jnp.where(pre > 0, pre, ex - 1.0)
        deriv[i, pl.ds(pl.multiple_of(start + at, 8), count), :] = ex
        return jnp.sum(act, axis=0, keepdims=True) * (1.0 / EPOCH)

    pl.semaphore_wait(barrier, 19)

    def tell(sem, dev):
        pl.semaphore_signal(sem, inc=1, device_id=dev, device_id_type=MESH)

    def along_y(d):
        return (lax.rem(yy + d, ny), tm, xx)

    def along_z(d):
        return (yy, lax.rem(zz + d, nz) * 2 + cc, xx)

    partner = (yy, zz * 2 + oc, xx)
    pair_copies = []

    def to_partner(ref, rows, src=None):
        k = len(pair_copies)
        c = remote(ref.at[:, rows] if src is None else src, ref.at[:, rows], pair_send.at[k], pair_recv.at[k], partner)
        c.start()
        pair_copies.append(c)

    halo_src = pl.ds(pl.multiple_of(464 * cc, 16), PAD)
    halo_dst = pl.ds(pl.multiple_of((PAD + 960) * oc, 16), PAD)
    has_next = jnp.where(cc == 0, zz > 0, zz < nz - 1)
    halo_copies = [
        remote(
            x.at[:, halo_src], xc.at[:, halo_dst], halo_send.at[c], halo_recv.at[oc],
            (yy, (zz - 1 + 2 * cc) * 2 + c, xx),
        )
        for c in range(2)
    ]

    @pl.when(has_next)
    def _():
        for c in halo_copies:
            c.start()

    nearby = (2, 6, 1, 7)
    teach_copies = [
        remote(teach.at[yy], teach.at[yy], teach_send.at[k], teach_recv.at[yy], (lax.rem(yy + d, ny), tm, xx))
        for k, d in enumerate(nearby)
    ]
    for c in teach_copies:
        c.start()
    to_partner(xc, pl.ds(pl.multiple_of(480 + 16 * cc, 16), PAD), x.at[:, pl.ds(pl.multiple_of(464 * oc, 16), PAD)])
    for dev in (along_z(7), along_z(1), along_y(2), along_y(6)):
        tell(known1, dev)

    for c in loads:
        c.wait()
    for i in range(4):
        forward(i)
        for e, at, count in ((0, 8, EPOCH - 8), (1, EPOCH, EPOCH), (2, 2 * EPOCH, EPOCH), (3, 3 * EPOCH, EPOCH - 8)):
            pooled[pl.ds(4 * i + e, 1), :] = finish(i, at, count)

    to_partner(xc, pl.ds(pl.multiple_of(PAD + 496 * cc, 16), 464))
    to_partner(deriv, pl.ds(pl.multiple_of(start + 8, 8), 464))
    pair_copies[0].wait_recv()

    @pl.when(zz > 0)
    def _():
        arrived(xc.at[:, pl.ds(0, PAD)], halo_recv.at[0])

    @pl.when(zz < nz - 1)
    def _():
        arrived(xc.at[:, pl.ds(PAD + 960, PAD)], halo_recv.at[1])

    ends = [pl.ds(start, PAD), pl.ds(pl.multiple_of(start + PAD + 480, 16), PAD)]
    xh = jnp.concatenate([xc[i, r, :] for i in range(4) for r in ends], axis=0)
    for p in range(5):
        y = jnp.dot(xh, weights(p), preferred_element_type=f32)
        for i in range(4):
            for h, r in enumerate((0, PAD + 480)):
                o = (2 * i + h) * PAD
                y_taps[i, 2 * p, r : r + PAD, :] = y[o : o + PAD, :128]
                if p < 4:
                    y_taps[i, 2 * p + 1, r : r + PAD, :] = y[o : o + PAD, 128:]

    for i in range(4):
        for e, at in ((0, 0), (3, 472)):
            pooled[pl.ds(4 * i + e, 1), :] += finish(i, at, 8)

    for c in small[2:]:
        c.wait()
    cwt = cw[...]
    pool = pooled[...]
    part = jnp.zeros((8, 128), f32)
    for s in range(5):
        t = jnp.sum(pool * cwt[s : s + 1, :], axis=1, keepdims=True)
        part = jnp.where(lane[0:8] == s, t[0:8], part)
        part = jnp.where(lane[0:8] == 16 + s, t[8:16], part)
    logit[cc, xx] = part
    logit_copies = []
    for d in (2, 1, 3, 0):
        for c in range(2):
            if d:
                dev = (yy, zz * 2 + c, lax.rem(xx + d, nx))
            elif c == 0:
                dev = partner
            else:
                continue
            k = len(logit_copies)
            logit_copies.append(
                remote(logit.at[cc, xx], logit.at[cc, xx], logit_send.at[k], logit_recv.at[cc, xx], dev)
            )
    for c in logit_copies:
        c.start()

    to_partner(deriv, pl.ds(start, 8))
    to_partner(deriv, pl.ds(pl.multiple_of(start + 472, 8), 8))


    pair_copies[1].wait_recv()
    for i in range(4):
        xt[i] = xc[i].T
    pl.semaphore_wait(known1, 4)
    for dev in (along_z(6), along_z(2)):
        tell(known2, dev)
    for d in nearby:
        s = lax.rem(yy + d, ny)
        arrived(teach.at[s], teach_recv.at[s])
    nights = [night[i].astype(f32) for i in range(4)]
    lane8 = lane[0:8]
    sums = [jnp.zeros((8, 128), f32) for _ in range(4)]
    for d in (0, *nearby):
        t = teach[lax.rem(yy + d, ny)]
        of = jnp.where(lane8 < 16, t[:, 8:9], t[:, 24:25])
        for i in range(4):
            sums[i] = sums[i] + jnp.where(of == nights[i], t, 0.0)
    soft = []
    for i in range(4):
        s = sums[i] + pltpu.roll(sums[i], 112, 1)
        s = s[0:4] + s[4:8]
        soft.append(s / s[:, 9:10])
    soft = jnp.concatenate(soft, axis=0)
    label = jnp.zeros((16, 128), i32)
    for i in range(4):
        for e in range(4):
            label = jnp.where(row == 4 * i + e, labels[e, night[i]], label)
    goal[cc] = 0.5 * soft + 0.5 * (lane == label).astype(f32)
    goal_copy = remote(goal.at[cc], goal.at[cc], pair_send.at[5], pair_recv.at[5], partner)
    goal_copy.start()

    for d in range(1, 4):
        s = lax.rem(xx + d, nx)
        for c in range(2):
            arrived(logit.at[c, s], logit_recv.at[c, s])
    arrived(logit.at[oc, xx], logit_recv.at[oc, xx])
    goal_copy.wait_recv()
    shift = jnp.zeros((16, 128), f32)
    for s in range(5):
        shift = shift + jnp.where(lane == s, bias[s], 0.0)
    slopes, both = [], []
    for b in range(2):
        logits = logit[b, 0] + logit[b, 1] + logit[b, 2] + logit[b, 3]
        logits = jnp.concatenate([logits, pltpu.roll(logits, 112, 1)], axis=0) + shift
        both.append(logits)
        expo = jnp.where(lane < 5, jnp.exp(logits), 0.0)
        diff = expo / jnp.sum(expo, axis=1, keepdims=True) - goal[b]
        slope = jnp.zeros((16, 128), f32)
        for s in range(5):
            slope = slope + diff[:, s : s + 1] * cwt[s : s + 1, :]
        slopes.append(slope)
    logits = jnp.where(cc == 0, both[0], both[1])
    for i in range(4):
        logits_out[i] = logits[4 * i : 4 * i + 4, :5]

    for c in pair_copies[2:]:
        c.wait_recv()
    for i in range(4):
        for b in range(2):
            for e in range(4):
                o = 480 * b + EPOCH * e
                up[i, pl.ds(24 + o, EPOCH), :] = (
                    deriv[i, pl.ds(o, EPOCH), :] * slopes[b][4 * i + e : 4 * i + e + 1, :]
                )

    def backward(taps, channels, at):
        acc = None
        for i in range(4):
            us = [up[i, pl.ds(12 - k, LONG), :].astype(bf16) for k in taps]
            u = us[0] if len(us) == 1 else jnp.concatenate(us, axis=1)
            g = jnp.dot(xt[i, channels, :], u, preferred_element_type=f32)
            acc = g if acc is None else acc + g
        for n in range(len(taps)):
            grad[pl.ds(at + acc.shape[0] * n, acc.shape[0]), :] = acc[:, 128 * n : 128 * n + 128]

    @pl.when(cc == 0)
    def _():
        backward((0, 1), slice(None), 0)
        backward((2, 3), slice(None), 512)
        backward((4,), slice(0, 128), 1024)

    @pl.when(cc == 1)
    def _():
        backward((4,), slice(128, 256), 0)
        backward((5, 6), slice(None), 128)
        backward((7, 8), slice(None), 640)

    power = jnp.ceil(jnp.log2(jnp.maximum(jnp.max(jnp.abs(grad[...]), axis=0, keepdims=True), 1e-30)) + 0.01)
    factor = jnp.exp2(15.0 - power)
    power = jnp.broadcast_to(power, (8, 128))

    def code(slot, units):
        t = jnp.concatenate([grad[pl.ds(288 * y + UNIT * z, UNIT), :] for y, z in units], axis=0)
        tx[slot] = jnp.concatenate([jnp.round(t * factor), power], axis=0).astype(i32).astype(i16)

    pl.semaphore_wait(known2, 2)
    half_y, half_z = yy // 4 == cc, zz // 4
    copies = []

    def send(copy, sent):
        copies.append((copy, sent))
        copy.start() if sent is True else pl.when(sent)(copy.start)

    far_first = ((2, 0), (3, 1), (1, 3), (0, 2))
    for h in range(2):
        for j in range(4):
            code(2 * j + h, [(j, j % 2 + 4 * h), (j, j % 2 + 4 * h + 2)])
        for m, (near, far) in enumerate(far_first):
            j = lax.rem(yy + jnp.where(half_y, near, far), 4)
            dev = (4 * cc + j, zz * 2 + (oc if h else cc), xx)
            send(
                remote(tx.at[2 * j + h], rx.at[yy], send1.at[4 * h + m], recv1.at[yy], dev),
                True if h else yy != 4 * cc + j,
            )
        for z in range(4 * h, 4 * h + 4):
            code(8 + z, [(1 - z % 2, z), (3 - z % 2, z)])
        for m, (near, far) in enumerate(far_first):
            z = 4 * h + lax.rem(zz + jnp.where(half_z == h, near, far), 4)
            dev = (yy, z * 2 + cc, xx)
            send(
                remote(tx.at[8 + z], rx.at[8 + zz], send1.at[8 + 4 * h + m], recv1.at[8 + zz], dev),
                zz != z,
            )

    @pl.when(half_y)
    def _():
        rx[yy] = tx[2 * lax.rem(yy, 4)]

    rx[8 + zz] = tx[8 + zz]

    handed = []
    for k in range(2):
        for m in range(4):
            if k == 0:
                own, dev = zz, (yy, (yy % 2 + jnp.where(half_y, 0, 4) + 2 * (m // 2)) * 2 + m % 2, xx)
            else:
                own, dev = yy, (4 * cc + 1 - zz % 2 + 2 * (m // 2), zz * 2 + m % 2, xx)
            slot = 4 * k + m
            copy = remote(tx2.at[slot], rx2.at[own], send2.at[slot], recv2.at[own], dev)
            handed.append((copy, (dev[0] != yy) | (dev[1] != tm), own))

    def hand_out(k):
        acc = jnp.zeros((WIDE, 128), f32)
        for s in range(8):
            if k == 0:
                @pl.when(jnp.logical_not(half_y & (yy == s)))
                def _():
                    arrived(rx.at[s], recv1.at[s])
            else:
                @pl.when(zz != s)
                def _():
                    arrived(rx.at[8 + s], recv1.at[8 + s])
        for s in range(8 * k, 8 * k + 8):
            t = rx[s].astype(f32)
            acc = acc + t[:WIDE] * jnp.exp2(t[WIDE : WIDE + 1] - 15.0)
        piece[0:WIDE, :] = acc
        piece[WIDE:, :] = jnp.zeros((8, 128), f32)
        for slot in range(4 * k, 4 * k + 4):
            copy, sent, own = handed[slot]
            tx2[slot] = piece[pl.ds(18 * (slot % 4), 24), :]
            pl.when(sent)(copy.start)

            @pl.when(jnp.logical_not(sent))
            def _():
                rx2[own] = tx2[slot]

    z_first = jnp.logical_not(half_y) | (zz < 4)

    @pl.when(jnp.logical_not(z_first))
    def _():
        hand_out(0)
        hand_out(1)

    @pl.when(z_first)
    def _():
        hand_out(1)
        hand_out(0)

    copies += [(copy, sent) for copy, sent, _ in handed]
    even = (yy + zz) % 2 == 0
    holder = jnp.where(even & (half_z == 1), 1 - yy // 4, yy // 4)
    place = jnp.where(even, zz, yy)
    for s in range(8):
        @pl.when(jnp.logical_not((place == s) & (holder == cc)))
        def _():
            arrived(rx2.at[s], recv2.at[s])
    out = rx2[0]
    for s in range(1, 8):
        out = out + rx2[s]
    grad_out[...] = out[:18] * (1.0 / 32)

    @pl.when(has_next)
    def _():
        for c in halo_copies:
            c.wait_send()

    for c in pair_copies + [goal_copy] + teach_copies + logit_copies:
        c.wait_send()
    for c, sent in copies:
        c.wait_send() if sent is True else pl.when(sent)(c.wait_send)


def local(activations, conv_weight, class_weight, class_bias, teacher_logits, night_of, section_labels):
    hbm = pl.BlockSpec(memory_space=pltpu.HBM)
    vm = pl.BlockSpec(memory_space=pltpu.VMEM)
    dma = pltpu.SemaphoreType.DMA
    return pl.pallas_call(
        kernel,
        out_shape=(pltpu.VMEM((4, 4, 5), f32), pltpu.VMEM((18, 128), f32)),
        in_specs=[hbm] * 7,
        out_specs=(vm, vm),
        scratch_shapes=[
            pltpu.VMEM((5, 128), f32),
            pltpu.VMEM((4, 4, 5), f32),
            pltpu.SMEM((4,), i32),
            pltpu.SMEM((4, 8), i32),
            pltpu.SMEM((5,), f32),
            pltpu.VMEM((4, LONG, 256), bf16),
            pltpu.VMEM((2304, 128), bf16),
            pltpu.VMEM((4, 9, 512, 128), f32),
            pltpu.VMEM((4, 960, 128), f32),
            pltpu.VMEM((16, 128), f32),
            pltpu.VMEM((4, LONG + 16, 128), f32),
            pltpu.VMEM((4, 256, LONG), bf16),
            pltpu.VMEM((1152, 128), f32),
            pltpu.VMEM((8, 8, 128), f32),
            pltpu.VMEM((2, 16, 128), f32),
            pltpu.VMEM((2, 4, 8, 128), f32),
            pltpu.VMEM((16, WIDE + 8, 128), i16),
            pltpu.VMEM((16, WIDE + 8, 128), i16),
            pltpu.VMEM((WIDE + 8, 128), f32),
            pltpu.VMEM((8, 24, 128), f32),
            pltpu.VMEM((8, 24, 128), f32),
            dma((5,)), dma((5,)),
            dma((2,)), dma((2,)),
            dma((6,)), dma((6,)),
            dma((4,)), dma((8,)),
            dma((7,)), dma((2, 4)),
            dma((16,)), dma((16,)),
            dma((8,)), dma((8,)),
            pltpu.SemaphoreType.REGULAR, pltpu.SemaphoreType.REGULAR,
        ],
        compiler_params=pltpu.CompilerParams(
            collective_id=0, has_side_effects=True, vmem_limit_bytes=63 << 20
        ),
    )(activations, conv_weight, class_weight.T, teacher_logits, night_of, section_labels.T, class_bias)


def solution(mesh):
    in_specs = (
        P("inst", "tm", None),
        P(None, "filt"),
        P("filt", None),
        P(),
        P("inst", "tm", None),
        P("inst"),
        P(None, "tm"),
    )
    out_specs = (P("inst", "tm", None), P(("inst", "tm"), "filt"))
    return jax.shard_map(local, mesh=mesh, in_specs=in_specs, out_specs=out_specs, check_vma=False)
```
